128 devices in a mesh: member: 8 (over z_hi, y), domain: 16 (over x, z_lo, core).
Axes of the slice: x: 4, y: 4, z: 4 (z_hi: 2, z_lo: 2; z = z_hi * 2 + z_lo), core: 2. Of those that a mesh axis runs over, the one named last changes fastest.
Arguments:
- ensemble: float32 [32, 3, 4, 2048, 128], P('member', None, None, 'domain'), may hold values from -6 to 6
- control: float32 [8, 3, 4, 2048, 128], P('member', None, None, 'domain'), may hold values from -6 to 6
- owner: int32 [16], replicated, may hold values from 0 to 7
- neighbours: int32 [16, 4], replicated, may hold values from 0 to 15
- edge_codes: int32 [16, 4], replicated, may hold values from 0 to 7
Outputs:
- advanced: float32 [32, 3, 4, 2048, 128], P('member', None, None, 'domain')
The draws below stay inside these ranges and needn't reach their ends.
Inputs may be any that keep to these rules, and one draw needn't show every extreme that they name: `owner`: one member position for each patch. `neighbours`: index of a patch. `edge_codes`: side code plus 4 if reversed.
All inputs are finite; a program needn't handle non-finite values.
Results may differ from the reference program's by a relative error of at most 0.0003.
Values sent between devices are 32-bit elements; how exact they have to be, the bound alone decides.
No kernel may reach another device: no remote copies, remote signals or barrier semaphores. Data moves between devices by JAX's collectives and lax.ppermute only.
A program may use at most 64 MiB of HBM per device.

```python
import jax
import jax.numpy as jnp
from jax import lax

PATCH = 128
LEV = 4
FIELDS = 3
MEMBERS = 32
ROWS = 2048
N_MEMBER = 8
N_DOMAIN = 16


def touch_ends(values, stream_key, low, largest):
    longest = values.shape.index(max(values.shape))
    spots = []
    for shift in (0, 1):
        where = [jax.random.randint(jax.random.fold_in(stream_key, axis), (), 0, length) for axis, length in enumerate(values.shape)]
        where[longest] = (where[longest] + shift) % values.shape[longest]
        spots.append(tuple(where))
    return values.at[spots[0]].set(low).at[spots[1]].set(largest)


def shard_levels(stream_key, dims, shards, least, top_value):
    def one(dim, blocks):
        steps = jax.random.uniform(jax.random.fold_in(jax.random.fold_in(stream_key, 6), dim), (blocks,), jnp.float32, least / len(shards), top_value / len(shards))
        return jnp.repeat(jnp.exp(steps), dims[dim] // blocks).reshape((-1,) + (1,) * (len(dims) - dim - 1))

    loudness = one(*shards[0])
    for cut in shards[1:]:
        loudness = loudness * one(*cut)
    return loudness


def scatter_about(own_key, dims, deviation, reach, pieces=(), kind=jnp.bfloat16):
    drawn = jax.random.normal(own_key, dims, jnp.float32) * deviation
    if len(pieces) > 0:
        drawn = shard_levels(own_key, dims, pieces, -0.22, 0.18) * drawn
    return jnp.clip(drawn, min=-reach, max=reach).astype(kind)


def setup_inputs(seed: int = 0) -> dict:
    seeds = jax.random.split(jax.random.key(seed), 6)
    ensemble = scatter_about(seeds[0], (MEMBERS, FIELDS, LEV, ROWS, PATCH), 1.0, 6.0, ((0, 8), (3, 16)), jnp.float32)
    control = scatter_about(seeds[1], (N_MEMBER, FIELDS, LEV, ROWS, PATCH), 1.0, 6.0, ((0, 8), (3, 16)), jnp.float32)
    owner = touch_ends(jax.random.randint(seeds[2], (N_DOMAIN,), 0, N_MEMBER), jax.random.fold_in(seeds[2], 1), 0, N_MEMBER - 1).astype(jnp.int32)
    neighbours = touch_ends(jax.random.randint(seeds[3], (N_DOMAIN, 4), 0, N_DOMAIN), jax.random.fold_in(seeds[3], 1), 0, N_DOMAIN - 1).astype(jnp.int32)
    edge_codes = touch_ends(jax.random.randint(seeds[4], (N_DOMAIN, 4), 0, 8), jax.random.fold_in(seeds[4], 1), 0, 7).astype(jnp.int32)
    return {"ensemble": ensemble, "control": control, "owner": owner, "neighbours": neighbours, "edge_codes": edge_codes}


def edge_strips(field):
    size = field.shape[-1]
    top = field[..., 0:2, :]
    bottom = jnp.flip(field[..., size - 2:, :], axis=-2)
    left = jnp.swapaxes(field[..., :, 0:2], -1, -2)
    right = jnp.swapaxes(jnp.flip(field[..., :, size - 2:], axis=-1), -1, -2)
    return jnp.stack([top, bottom, left, right], axis=0)


def pick_rims(strips_all, neigh_row, code_row):
    chosen = []
    for border in range(4):
        source = strips_all[neigh_row[border], code_row[border] % 4]
        flipped = jnp.flip(source, axis=-1)
        chosen.append(jnp.where(code_row[border] // 4 == 1, flipped, source))
    return chosen


def assemble(center, rims):
    top, bottom, left, right = rims
    middle = jnp.concatenate([jnp.flip(jnp.swapaxes(left, -1, -2), axis=-1), center, jnp.swapaxes(right, -1, -2)], axis=-1)
    zeros = jnp.zeros(top.shape[:-1] + (2,), center.dtype)
    upper = jnp.concatenate([zeros, jnp.flip(top, axis=-2), zeros], axis=-1)
    lower = jnp.concatenate([zeros, bottom, zeros], axis=-1)
    return jnp.concatenate([upper, middle, lower], axis=-2)


def stencil_step(padded):
    wind_x = padded[..., 0, :, :, :]
    wind_y = padded[..., 1, :, :, :]
    divergence = 0.5 * (wind_x[..., 1:-1, 2:] - wind_x[..., 1:-1, :-2] + wind_y[..., 2:, 1:-1] - wind_y[..., :-2, 1:-1])
    center = padded[..., 2:-2, 2:-2]
    diff_x = padded[..., 2:-2, 3:-1] - padded[..., 2:-2, 1:-3]
    diff_y = padded[..., 3:-1, 2:-2] - padded[..., 1:-3, 2:-2]
    center_x = center[..., 0:1, :, :, :]
    center_y = center[..., 1:2, :, :, :]
    moved = center - 0.2 * (center_x * diff_x + center_y * diff_y)
    grad_x = divergence[..., 1:-1, 2:] - divergence[..., 1:-1, :-2]
    grad_y = divergence[..., 2:, 1:-1] - divergence[..., :-2, 1:-1]
    first = moved[..., 0, :, :, :] + 0.1 * grad_x
    second = moved[..., 1, :, :, :] + 0.1 * grad_y
    return jnp.stack([first, second, moved[..., 2, :, :, :]], axis=-4)


def reference(ensemble, control, owner, neighbours, edge_codes):
    mean = jnp.sum(ensemble, axis=0) / MEMBERS
    count, fields, levels, rows, width = ensemble.shape
    control_tiles = control.reshape(N_MEMBER, fields, levels, N_DOMAIN, PATCH, PATCH)
    patch_ids = jnp.arange(N_DOMAIN, dtype=jnp.int32)
    picked = control_tiles[owner, :, :, patch_ids]
    picked = jnp.moveaxis(picked, 0, 2).reshape(fields, levels, rows, width)
    shift = picked - mean
    recentered = ensemble + shift[None]
    tiles = recentered.reshape(count, fields, levels, N_DOMAIN, PATCH, PATCH)
    tiles = jnp.moveaxis(tiles, 3, 0)
    strips_all = jnp.moveaxis(edge_strips(tiles), 1, 0)

    def one_tile(position):
        chosen = pick_rims(strips_all, neighbours[position], edge_codes[position])
        return stencil_step(assemble(tiles[position], chosen))

    result = lax.map(one_tile, jnp.arange(N_DOMAIN, dtype=jnp.int32))
    return jnp.moveaxis(result, 0, 3).reshape(count, fields, levels, rows, width)
```

```python
import jax
import jax.numpy as jnp
from jax import lax
from jax.experimental import pallas as pl
from jax.experimental.pallas import tpu as pltpu
from jax.sharding import PartitionSpec as P

MESH = ("member", "domain")
N_MEMBER = 8
N_DOMAIN = 16
SIZE = 128
PLANES = 12
LEV = 4
LOCAL = 4
MEMBERS = 32
ROWS = PLANES * SIZE
CHUNK = ROWS // N_MEMBER
OFFSETS = ((6, 5, 1, 0), (7, 4, 3, 2))
EDGE = 24
STRIP = 4 * EDGE
F32 = jnp.float32


def pairs(target):
    out = []
    for m in range(N_MEMBER):
        for d in range(N_DOMAIN):
            to = target(m, d)
            if to is not None:
                out.append((m * N_DOMAIN + d, to[0] * N_DOMAIN + to[1]))
    return out


def send(array, target):
    return lax.ppermute(array, MESH, pairs(target))


def swap_cores(array):
    return send(array, lambda m, d: (m, d ^ 1))


def exchange(messages):
    out = []
    for j, message in enumerate(messages):

        def target(m, d, j=j):
            offset = OFFSETS[d % 2][j]
            return (m ^ offset, d) if offset else None

        out.append(send(message, target))
    return out


def vmem():
    return pl.BlockSpec(memory_space=pltpu.VMEM)


def smem():
    return pl.BlockSpec(memory_space=pltpu.SMEM)


def hbm():
    return pl.BlockSpec(memory_space=pl.ANY)


def shaped(*shape):
    return jax.ShapeDtypeStruct(shape, F32)


def slot_chunk(member, core, j):
    zero, one = OFFSETS[0][j % 4], OFFSETS[1][j % 4]
    if j >= 4:
        zero, one = one, zero
    return member ^ jnp.where(core == 0, zero, one)


def prepare_kernel(place, owner, ens_hbm, ctl_hbm, keep, give, strips, ens, ctl, part, tile, turned, sems):
    member, patch = place[0], place[1]
    core = patch % 2
    flag = jnp.where(owner[patch] == member, 1.0, 0.0).astype(F32)
    copies = []
    for i in range(PLANES):
        a = pltpu.make_async_copy(ens_hbm.at[:, i], ens.at[:, i], sems.at[0, i])
        b = pltpu.make_async_copy(ctl_hbm.at[i], ctl.at[i], sems.at[1, i])
        a.start()
        b.start()
        copies.append((a, b))
    for i in range(PLANES):
        for c in copies[i]:
            c.wait()
        for r in range(0, SIZE, 32):
            rows = pl.ds(r, 32)
            lane = lax.broadcasted_iota(jnp.int32, (32, SIZE), 1)
            group = lane // 4
            xs = [ens[a, i, rows, :] for a in range(LOCAL)]
            total = (xs[0] + xs[1]) + (xs[2] + xs[3])
            value = flag * ctl[i, rows, :] - total * (1.0 / MEMBERS)
            part[pl.ds(i * SIZE + r, 32), :] = value
            spots = [a * PLANES + i for a in range(LOCAL)] + [LOCAL * PLANES + i]
            for t in (0, 1):
                mine = [(s % 32, x) for s, x in zip(spots, xs + [value]) if s // 32 == t]
                if not mine:
                    continue
                acc = tile[t, rows, :]
                for s, x in mine:
                    acc = jnp.where(group == s, pltpu.roll(x, (4 * s + 2) % SIZE, 1), acc)
                tile[t, rows, :] = acc
        for a in range(LOCAL):
            s = a * PLANES + i
            strips[s : s + 1, :] = ens[a, i, 0:1, :]
            strips[48 + s : 49 + s, :] = ens[a, i, 1:2, :]
            strips[96 + s : 97 + s, :] = ens[a, i, SIZE - 1 : SIZE, :]
            strips[144 + s : 145 + s, :] = ens[a, i, SIZE - 2 : SIZE - 1, :]
        base, row = 4 * CHUNK, i * SIZE
        give[base + i : base + i + 1, :] = part[row : row + 1, :]
        give[base + 12 + i : base + 13 + i, :] = part[row + 1 : row + 2, :]
        give[base + 24 + i : base + 25 + i, :] = part[row + SIZE - 1 : row + SIZE, :]
        give[base + 36 + i : base + 37 + i, :] = part[row + SIZE - 2 : row + SIZE - 1, :]
    turned[0] = tile[0].T
    turned[1] = tile[1].T
    for side, k, q in ((2, 0, 2), (2, 1, 3), (3, 0, 1), (3, 1, 0)):
        at = side * 96 + k * 48
        strips[at : at + 32, :] = turned[0, pl.ds(q, 32, stride=4), :]
        strips[at + 32 : at + 48, :] = turned[1, pl.ds(q, 16, stride=4), :]
        at = 4 * CHUNK + side * EDGE + k * PLANES
        give[at : at + PLANES, :] = turned[1, pl.ds(64 + q, PLANES, stride=4), :]
    for j in range(4):
        own = pl.multiple_of(slot_chunk(member, core, j) * CHUNK, 8)
        other = pl.multiple_of(slot_chunk(member, core, j + 4) * CHUNK, 8)
        keep[j * CHUNK : (j + 1) * CHUNK, :] = part[pl.ds(own, CHUNK), :]
        give[j * CHUNK : (j + 1) * CHUNK, :] = part[pl.ds(other, CHUNK), :]


def prepare(place, owner, ensemble, control):
    return pl.pallas_call(
        prepare_kernel,
        out_shape=[shaped(4 * CHUNK, SIZE), shaped(4 * CHUNK + STRIP, SIZE), shaped(4 * 96, SIZE)],
        in_specs=[smem(), smem(), hbm(), hbm()],
        out_specs=[vmem()] * 3,
        scratch_shapes=[
            pltpu.VMEM((LOCAL, PLANES, SIZE, SIZE), F32),
            pltpu.VMEM((PLANES, SIZE, SIZE), F32),
            pltpu.VMEM((ROWS, SIZE), F32),
            pltpu.VMEM((2, SIZE, SIZE), F32),
            pltpu.VMEM((2, SIZE, SIZE), F32),
            pltpu.SemaphoreType.DMA((2, PLANES)),
        ],
        compiler_params=pltpu.CompilerParams(vmem_limit_bytes=16 << 20),
        cost_estimate=pl.CostEstimate(flops=2_000_000, bytes_accessed=5_000_000, transcendentals=0),
        name="prepare",
    )(place, owner, ensemble, control)


def pack_kernel(keep, give, got, m0, m1, m2, m3, edges):
    for j, m in enumerate((m0, m1, m2, m3)):
        m[0:CHUNK, :] = keep[j * CHUNK : (j + 1) * CHUNK, :]
        m[CHUNK:, :] = got[j * CHUNK : (j + 1) * CHUNK, :]
    edges[0:STRIP, :] = give[4 * CHUNK :, :]
    edges[STRIP:, :] = got[4 * CHUNK :, :]


def pack(keep, give, got):
    return pl.pallas_call(
        pack_kernel,
        out_shape=[shaped(2 * CHUNK, SIZE)] * 4 + [shaped(2 * STRIP, SIZE)],
        in_specs=[vmem()] * 3,
        out_specs=[vmem()] * 5,
        name="pack",
    )(keep, give, got)


def add_kernel(place, a, b, c, d, own, out):
    first = place[1] % 2 == 0
    out[...] = (a[...] + b[...]) + (c[...] + jnp.where(first, own[...], d[...]))


def add(place, received, own):
    return pl.pallas_call(
        add_kernel,
        out_shape=shaped(2 * CHUNK, SIZE),
        in_specs=[smem()] + [vmem()] * 5,
        out_specs=vmem(),
        name="add",
    )(place, *received, own)


def flipped(x, turn):
    lane = lax.broadcasted_iota(jnp.int32, x.shape, 1)
    return jnp.take_along_axis(x, jnp.where(turn, SIZE - 1 - lane, lane), axis=1)


def reduce_kernel(place, neighbours, codes, acc, sib, g0, g1, g2, g3, out):
    out[0:CHUNK, :] = acc[0:CHUNK, :] + sib[CHUNK:, :]
    out[CHUNK : 2 * CHUNK, :] = acc[CHUNK:, :] + sib[0:CHUNK, :]
    patch = place[1]
    for q in (0, 1):
        for side in range(4):
            code = codes[patch ^ q, side]
            away = neighbours[patch ^ q, side] ^ patch
            x_away = away // 4
            at = pl.multiple_of((away % 4) * STRIP + (code % 4) * EDGE, 8)
            picked = g0[pl.ds(at, EDGE), :]
            for x, g in ((1, g1), (2, g2), (3, g3)):
                picked = jnp.where(x_away == x, g[pl.ds(at, EDGE), :], picked)
            to = 2 * CHUNK + q * STRIP + side * EDGE
            out[to : to + EDGE, :] = flipped(picked, code // 4 == 1)


def reduce(place, neighbours, codes, acc, sib, groups):
    return pl.pallas_call(
        reduce_kernel,
        out_shape=shaped(2 * CHUNK + 2 * STRIP, SIZE),
        in_specs=[smem()] * 3 + [vmem()] * 6,
        out_specs=vmem(),
        name="reduce",
    )(place, neighbours, codes, acc, sib, *groups)


def share_kernel(place, a, b, c, d, own, out):
    first = place[1] % 2 == 0
    for j, m in enumerate((a, b, c)):
        out[j * CHUNK : (j + 1) * CHUNK, :] = m[CHUNK : 2 * CHUNK, :]
    out[3 * CHUNK : 4 * CHUNK, :] = jnp.where(first, own[CHUNK : 2 * CHUNK, :], d[CHUNK : 2 * CHUNK, :])
    rows = pl.ds(2 * CHUNK + STRIP, STRIP)
    out[4 * CHUNK :, :] = (a[rows, :] + b[rows, :]) + (c[rows, :] + jnp.where(first, own[rows, :], d[rows, :]))


def share(place, received, own):
    return pl.pallas_call(
        share_kernel,
        out_shape=shaped(4 * CHUNK + STRIP, SIZE),
        in_specs=[smem()] + [vmem()] * 5,
        out_specs=vmem(),
        name="share",
    )(place, *received, own)


def slope(x):
    lane = lax.broadcasted_iota(jnp.int32, x.shape, 1)
    ahead = jnp.where(lane == SIZE - 1, 0.0, pltpu.roll(x, SIZE - 1, 1))
    behind = jnp.where(lane == 0, 0.0, pltpu.roll(x, 1, 1))
    return ahead - behind


def advance_kernel(place, neighbours, codes, ens, e0, e1, e2, e3, a, b, c, d, own, got, out,
                   shift, rims, lines, columns, pad, div, slope_u):
    member, patch = place[0], place[1]
    core = patch % 2
    step = pl.program_id(0)

    @pl.when(step == 0)
    def _():
        first = core == 0
        for j, m in enumerate((a, b, c, d)):
            value = m[0:CHUNK, :]
            if j == 3:
                value = jnp.where(first, own[0:CHUNK, :], value)
            shift[pl.ds(pl.multiple_of(slot_chunk(member, core, j) * CHUNK, 8), CHUNK), :] = value
            at = pl.multiple_of(slot_chunk(member, core, j + 4) * CHUNK, 8)
            shift[pl.ds(at, CHUNK), :] = got[j * CHUNK : (j + 1) * CHUNK, :]
        for side, e in enumerate((e0, e1, e2, e3)):
            turn = codes[patch, side] // 4 == 1
            rows = pl.ds(2 * CHUNK + side * EDGE, EDGE)
            moved = (a[rows, :] + b[rows, :]) + (c[rows, :] + jnp.where(first, own[rows, :], d[rows, :]))
            moved = moved + got[4 * CHUNK + side * EDGE : 4 * CHUNK + (side + 1) * EDGE, :]
            strip = flipped(e[0, 0], turn)
            for k in (0, 1):
                for n in range(LOCAL):
                    at = k * 48 + n * PLANES
                    rims[n, side * 2 + k, 0:PLANES, :] = strip[at : at + PLANES, :] + moved[k * PLANES : (k + 1) * PLANES, :]
        for n in range(LOCAL):
            at = n * 32
            lines[pl.ds(at, PLANES, stride=2), :] = rims[n, 6, 0:PLANES, :]
            lines[pl.ds(at + 1, PLANES, stride=2), :] = rims[n, 4, 0:PLANES, :]
            right = 0.5 * (rims[n, 7, 0:LEV, :] + slope(rims[n, 6, LEV : 2 * LEV, :]))
            left = 0.5 * (slope(rims[n, 4, LEV : 2 * LEV, :]) - rims[n, 5, 0:LEV, :])
            lines[pl.ds(at + 24, LEV, stride=2), :] = right
            lines[pl.ds(at + 25, LEV, stride=2), :] = left
        turned = lines[...].T
        for n in range(LOCAL):
            columns[n] = turned if n == 0 else pltpu.roll(turned, SIZE - 32 * n, 1)

    part = 32
    lane = lax.broadcasted_iota(jnp.int32, (part, SIZE), 1)
    at_left, at_right = lane == 0, lane == SIZE - 1

    def across(x, r, line):
        edge = pltpu.roll(columns[step, r : r + part, :], (SIZE - 1 - 2 * line) % SIZE, 1)
        return jnp.where(at_right, edge, pltpu.roll(x, SIZE - 1, 1)) - jnp.where(at_left, edge, pltpu.roll(x, 1, 1))

    for lev in range(LEV):
        for f in range(3):
            i = f * LEV + lev
            pad[f, 8 : 8 + SIZE, :] = ens[0, i] + shift[i * SIZE : (i + 1) * SIZE, :]
            pad[f, 7:8, :] = rims[step, 0, i : i + 1, :]
            pad[f, 8 + SIZE : 9 + SIZE, :] = rims[step, 2, i : i + 1, :]
        i = LEV + lev
        div[7:8, :] = 0.5 * (slope(pad[0, 7:8, :]) + pad[1, 8:9, :] - rims[step, 1, i : i + 1, :])
        div[8 + SIZE : 9 + SIZE, :] = 0.5 * (
            slope(pad[0, 8 + SIZE : 9 + SIZE, :]) + rims[step, 3, i : i + 1, :] - pad[1, 7 + SIZE : 8 + SIZE, :]
        )
        for r in range(0, SIZE, part):
            at = 8 + r
            du = across(pad[0, at : at + part, :], r, lev)
            slope_u[r : r + part, :] = du
            div[at : at + part, :] = 0.5 * (du + pad[1, at + 1 : at + 1 + part, :] - pad[1, at - 1 : at - 1 + part, :])
        for r in range(0, SIZE, part):
            at = 8 + r
            here = slice(at, at + part)
            up, down = slice(at - 1, at - 1 + part), slice(at + 1, at + 1 + part)
            u, v, w = pad[0, here, :], pad[1, here, :], pad[2, here, :]
            edge = pltpu.roll(columns[step, r : r + part, :], (SIZE - 1 - 2 * (PLANES + lev)) % SIZE, 1)
            edge = edge + jnp.where(at_left, 0.5 * u, -0.5 * u)
            mid = div[here, :]
            grad_x = jnp.where(at_right, edge, pltpu.roll(mid, SIZE - 1, 1)) - jnp.where(at_left, edge, pltpu.roll(mid, 1, 1))
            grad_y = div[down, :] - div[up, :]
            new_u = u - 0.2 * (u * slope_u[r : r + part, :] + v * (pad[0, down, :] - pad[0, up, :]))
            new_v = v - 0.2 * (u * across(v, r, LEV + lev) + v * (pad[1, down, :] - pad[1, up, :]))
            new_w = w - 0.2 * (u * across(w, r, 2 * LEV + lev) + v * (pad[2, down, :] - pad[2, up, :]))
            out[0, lev, r : r + part, :] = new_u + 0.1 * grad_x
            out[0, LEV + lev, r : r + part, :] = new_v + 0.1 * grad_y
            out[0, 2 * LEV + lev, r : r + part, :] = new_w


def advance(place, neighbours, codes, ensemble, gathered, received, own, got):
    def strip(side):
        def where(n, place, neighbours, codes):
            patch = place[1]
            return neighbours[patch, side], codes[patch, side] % 4, 0, 0

        return pl.BlockSpec((1, 1, 96, SIZE), where)

    block = pl.BlockSpec((1, PLANES, SIZE, SIZE), lambda n, *_: (n, 0, 0, 0))
    return pl.pallas_call(
        advance_kernel,
        out_shape=shaped(LOCAL, PLANES, SIZE, SIZE),
        grid_spec=pltpu.PrefetchScalarGridSpec(
            num_scalar_prefetch=3,
            grid=(LOCAL,),
            in_specs=[block] + [strip(s) for s in range(4)] + [vmem()] * 6,
            out_specs=block,
            scratch_shapes=[
                pltpu.VMEM((ROWS, SIZE), F32),
                pltpu.VMEM((LOCAL, 8, 16, SIZE), F32),
                pltpu.VMEM((SIZE, SIZE), F32),
                pltpu.VMEM((LOCAL, SIZE, SIZE), F32),
                pltpu.VMEM((3, SIZE + 16, SIZE), F32),
                pltpu.VMEM((SIZE + 16, SIZE), F32),
                pltpu.VMEM((SIZE, SIZE), F32),
            ],
        ),
        compiler_params=pltpu.CompilerParams(vmem_limit_bytes=24 << 20),
        cost_estimate=pl.CostEstimate(flops=40_000_000, bytes_accessed=8_000_000, transcendentals=0),
        name="advance",
    )(place, neighbours, codes, ensemble, *([gathered] * 4), *received, own, got)


def on_device(ensemble, control, owner, neighbours, codes):
    shape = ensemble.shape
    ensemble = ensemble.reshape(LOCAL, PLANES, SIZE, SIZE)
    control = control.reshape(PLANES, SIZE, SIZE)
    place = jnp.stack([lax.axis_index("member"), lax.axis_index("domain")]).astype(jnp.int32)

    keep, give, strips = prepare(place, owner, ensemble, control)
    gathered = lax.all_gather(strips, "domain", axis=0, tiled=True)
    gathered = gathered.reshape(N_DOMAIN, 4, 96, SIZE)

    got = swap_cores(give)
    *messages, edges = pack(keep, give, got)
    over_z = send(edges, lambda m, d: (m, d ^ 2))
    group = jnp.concatenate([edges, over_z], axis=0)
    received = exchange(messages)
    groups = [group] + [send(group, lambda m, d, x=x: (m, d ^ (4 * x))) for x in (1, 2, 3)]
    acc = add(place, received, messages[3])
    reduced = reduce(place, neighbours, codes, acc, swap_cores(acc), groups)
    received = exchange([reduced] * 4)
    got = swap_cores(share(place, received, reduced))
    out = advance(place, neighbours, codes, ensemble, gathered, received, reduced, got)
    return out.reshape(shape)


def solution(mesh):
    spec = P("member", None, None, "domain", None)
    return jax.shard_map(
        on_device, mesh=mesh, in_specs=(spec, spec, P(), P(), P()), out_specs=spec, check_vma=False
    )
```

```python
import jax
import jax.numpy as jnp
from jax import lax
from jax.experimental import pallas as pl
from jax.experimental.pallas import tpu as pltpu
from jax.sharding import PartitionSpec as P

MESH = ("member", "domain")
N_MEMBER = 8
N_DOMAIN = 16
SIZE = 128
PLANES = 12
LEV = 4
LOCAL = 4
MEMBERS = 32
ROWS = PLANES * SIZE
CHUNK = ROWS // N_MEMBER
OFFSETS = ((6, 5, 1, 0), (7, 4, 3, 2))
TAKEN = 20
SLOT = 32
RECORD = 4 * SLOT
USED = 16
STRIP = 4 * USED
MAIN = 4 * CHUNK
F32 = jnp.float32


def pairs(target):
    out = []
    for m in range(N_MEMBER):
        for d in range(N_DOMAIN):
            to = target(m, d)
            if to is not None:
                out.append((m * N_DOMAIN + d, to[0] * N_DOMAIN + to[1]))
    return out


def send(array, target):
    return lax.ppermute(array, MESH, pairs(target))


def swap_cores(array):
    return send(array, lambda m, d: (m, d ^ 1))


def exchange(messages, order=(0, 1, 2, 3)):
    out = [None] * 4
    for j in order:
        message = messages[j]

        def target(m, d, j=j):
            offset = OFFSETS[d % 2][j]
            return (m ^ offset, d) if offset else None

        out[j] = send(message, target)
    return out


def over_x(array):
    return [send(array, lambda m, d, x=x: (m, d ^ (4 * x))) for x in (1, 2, 3)]


def vmem():
    return pl.BlockSpec(memory_space=pltpu.VMEM)


def hbm():
    return pl.BlockSpec(memory_space=pltpu.HBM)


def shaped(*rows):
    return [jax.ShapeDtypeStruct((r, SIZE), F32) for r in rows]


def on(space, *arrays):
    return [pltpu.with_memory_space_constraint(x, space) for x in arrays]


def limit(mib):
    return pltpu.CompilerParams(vmem_limit_bytes=mib << 20)


def here():
    return lax.axis_index("member"), lax.axis_index("domain")


def slot_chunk(member, core, j):
    zero, one = OFFSETS[0][j % 4], OFFSETS[1][j % 4]
    if j >= 4:
        zero, one = one, zero
    return member ^ jnp.where(core == 0, zero, one)


def prepare_kernel(owner_hbm, ens_hbm, ctl_hbm, keep, give, stay, leave, ens, ctl, part, tile, turned, lines, edge, owner, sems, osem):
    member, patch = here()
    core, z = patch % 2, (patch // 2) % 2
    table = pltpu.make_async_copy(owner_hbm, owner, osem)
    table.start()
    copies = []
    for i in range(PLANES):
        a = pltpu.make_async_copy(ens_hbm.at[:, i], ens.at[:, i], sems.at[0, i])
        b = pltpu.make_async_copy(ctl_hbm.at[i], ctl.at[i], sems.at[1, i])
        a.start()
        b.start()
        copies.append((a, b))
    table.wait()
    flag = jnp.where(owner[patch] == member, 1.0, 0.0).astype(F32)
    for i in range(PLANES):
        for c in copies[i]:
            c.wait()
        spots = [(a // 2, (a % 2) * PLANES + i) for a in range(LOCAL)] + [(0, 24 + i) if i < 8 else (1, 16 + i)]
        for r in range(0, SIZE, 32):
            rows = pl.ds(r, 32)
            group = lax.broadcasted_iota(jnp.int32, (32, SIZE), 1) // 4
            xs = [ens[a, i, rows, :] for a in range(LOCAL)]
            total = (xs[0] + xs[1]) + (xs[2] + xs[3])
            value = flag * ctl[i, rows, :] - total * (1.0 / MEMBERS)
            part[pl.ds(i * SIZE + r, 32), :] = value
            for t in (0, 1):
                acc = tile[t, rows, :]
                for (where, s), x in zip(spots, xs + [value]):
                    if where == t:
                        acc = jnp.where(group == s, pltpu.roll(x, (4 * s + 2) % SIZE, 1), acc)
                tile[t, rows, :] = acc
        for side, k, row in ((0, 0, 0), (0, 1, 1), (1, 0, SIZE - 1), (1, 1, SIZE - 2)):
            at = k * PLANES + i
            if at < TAKEN:
                for a in range(LOCAL):
                    lines[a, side, at : at + 1, :] = ens[a, i, row : row + 1, :]
                edge[side, at : at + 1, :] = part[i * SIZE + row : i * SIZE + row + 1, :]
    turned[0] = tile[0].T
    turned[1] = tile[1].T
    for side, k, q in ((2, 0, 2), (2, 1, 3), (3, 0, 1), (3, 1, 0)):
        count = 8 if k else PLANES
        at = k * PLANES
        for a in range(LOCAL):
            lines[a, side, at : at + count, :] = turned[a // 2, pl.ds((a % 2) * 48 + q, count, stride=4), :]
        edge[side, at : at + 8, :] = turned[0, pl.ds(96 + q, 8, stride=4), :]
        if k == 0:
            edge[side, 8:12, :] = turned[1, pl.ds(96 + q, 4, stride=4), :]
    for out, who in ((stay, z), (leave, 1 - z)):
        for c in (0, 1):
            for side in range(4):
                at = c * RECORD + side * SLOT
                out[at : at + TAKEN, :] = lines[2 * c + who, side, 0:TAKEN, :]
                out[at + 20 : at + 30, :] = edge[side, 10 * c : 10 * c + 10, :]
                out[at + 30 : at + 32, :] = jnp.zeros((2, SIZE), F32)
    for j in range(4):
        own = pl.multiple_of(slot_chunk(member, core, j) * CHUNK, 8)
        other = pl.multiple_of(slot_chunk(member, core, j + 4) * CHUNK, 8)
        keep[j * CHUNK : (j + 1) * CHUNK, :] = part[pl.ds(own, CHUNK), :]
        give[j * CHUNK : (j + 1) * CHUNK, :] = part[pl.ds(other, CHUNK), :]


def prepare(owner, ensemble, control):
    return pl.pallas_call(
        prepare_kernel,
        out_shape=shaped(MAIN, MAIN, 2 * RECORD, 2 * RECORD),
        in_specs=[hbm()] * 3,
        out_specs=[vmem()] * 4,
        scratch_shapes=[
            pltpu.VMEM((LOCAL, PLANES, SIZE, SIZE), F32),
            pltpu.VMEM((PLANES, SIZE, SIZE), F32),
            pltpu.VMEM((ROWS, SIZE), F32),
            pltpu.VMEM((2, SIZE, SIZE), F32),
            pltpu.VMEM((2, SIZE, SIZE), F32),
            pltpu.VMEM((LOCAL, 4, 24, SIZE), F32),
            pltpu.VMEM((4, 24, SIZE), F32),
            pltpu.SMEM((N_DOMAIN,), jnp.int32),
            pltpu.SemaphoreType.DMA((2, PLANES)),
            pltpu.SemaphoreType.DMA,
        ],
        compiler_params=limit(12),
        cost_estimate=pl.CostEstimate(flops=2_000_000, bytes_accessed=5_000_000, transcendentals=0),
        name="prepare",
    )(*on(pltpu.HBM, owner, ensemble, control))


def small(kernel, name, rows, arrays):
    one = isinstance(rows, int)
    return pl.pallas_call(
        kernel,
        out_shape=shaped(rows)[0] if one else shaped(*rows),
        in_specs=[vmem()] * len(arrays),
        out_specs=vmem() if one else [vmem()] * len(rows),
        compiler_params=limit(4),
        name=name,
    )(*on(pltpu.VMEM, *arrays))


def pack_kernel(keep, got, m0, m1, m2, m3):
    for j, m in enumerate((m0, m1, m2, m3)):
        m[0:CHUNK, :] = keep[j * CHUNK : (j + 1) * CHUNK, :]
        m[CHUNK:, :] = got[j * CHUNK : (j + 1) * CHUNK, :]


def split_kernel(stay, came, out):
    _, patch = here()
    rows = pl.ds(pl.multiple_of((1 - patch % 2) * RECORD, 8), RECORD)
    out[0:RECORD, :] = stay[rows, :]
    out[RECORD:, :] = came[rows, :]


def group_kernel(stay, came, got, out):
    _, patch = here()
    rows = pl.ds(pl.multiple_of((patch % 2) * RECORD, 8), RECORD)
    out[0:RECORD, :] = stay[rows, :]
    out[RECORD : 2 * RECORD, :] = got[0:RECORD, :]
    out[2 * RECORD : 3 * RECORD, :] = came[rows, :]
    out[3 * RECORD :, :] = got[RECORD:, :]


def pick_kernel(table_hbm, g0, g1, g3, g2, stay, leave, half, table, sem):
    _, patch = here()
    copy = pltpu.make_async_copy(table_hbm, table, sem)
    copy.start()
    copy.wait()
    for q in range(4):
        to, base, rows = (stay, leave)[q // 2], (q % 2) * STRIP, SLOT if q < 2 else 24
        for side in range(4):
            spot = (patch ^ q) * 4 + side
            away = table[spot] ^ patch
            code = table[64 + spot]
            source = pl.ds(pl.multiple_of((away % 4) * RECORD + (code % 4) * SLOT, 8), rows)
            value = g0[source, :]
            for x, g in ((1, g1), (2, g2), (3, g3)):
                value = jnp.where(away // 4 == x, g[source, :], value)
            lane = lax.broadcasted_iota(jnp.int32, value.shape, 1)
            value = jnp.take_along_axis(value, jnp.where(code // 4 == 1, SIZE - 1 - lane, lane), axis=1)
            at, depth = base + side * USED, 16 if side < 2 else 12
            to[at : at + PLANES, :] = value[0:PLANES]
            to[at + PLANES : at + USED, :] = value[depth : depth + LEV]
            if q < 2:
                half[at : at + 10, :] = value[20:30]
                half[at + 10 : at + USED, :] = jnp.zeros((6, SIZE), F32)


def pick(table, g0, g1, g2, g3):
    return pl.pallas_call(
        pick_kernel,
        out_shape=shaped(*[2 * STRIP] * 3),
        in_specs=[hbm()] + [vmem()] * 4,
        out_specs=[vmem()] * 3,
        scratch_shapes=[pltpu.SMEM((128,), jnp.int32), pltpu.SemaphoreType.DMA],
        compiler_params=limit(4),
        name="pick",
    )(*on(pltpu.HBM, table), *on(pltpu.VMEM, g0, g1, g3, g2))


def add_kernel(a, b, c, d, own, out):
    _, patch = here()
    out[...] = (a[...] + b[...]) + (c[...] + jnp.where(patch % 2 == 0, own[...], d[...]))


def reduce_kernel(acc, sib, half, sib_half, out):
    _, patch = here()
    first = patch % 2 == 0
    out[0:CHUNK, :] = acc[0:CHUNK, :] + sib[CHUNK : 2 * CHUNK, :]
    out[CHUNK : 2 * CHUNK, :] = acc[CHUNK : 2 * CHUNK, :] + sib[0:CHUNK, :]
    for q in (0, 1):
        for side in range(4):
            at = q * STRIP + side * USED
            mine = half[at : at + USED, :]
            at = (1 - q) * STRIP + side * USED
            other = sib_half[at : at + USED, :]
            low, high = jnp.where(first, mine, other), jnp.where(first, other, mine)
            at, depth = 2 * CHUNK + q * STRIP + side * USED, 6 if side < 2 else 2
            out[at : at + 10, :] = low[0:10]
            out[at + 10 : at + 12, :] = high[0:2]
            out[at + 12 : at + 16, :] = high[depth : depth + LEV]


def share_kernel(own, d, c, b, a, stay, back, out):
    _, patch = here()
    first = patch % 2 == 0
    rows = slice(CHUNK, 2 * CHUNK)
    for j, m in enumerate((a, b, c)):
        out[j * CHUNK : (j + 1) * CHUNK, :] = m[rows, :]
    out[3 * CHUNK : 4 * CHUNK, :] = jnp.where(first, own[rows, :], d[rows, :])
    rows = slice(2 * CHUNK + STRIP, 2 * CHUNK + 2 * STRIP)
    out[MAIN : MAIN + STRIP, :] = (a[rows, :] + b[rows, :]) + (c[rows, :] + jnp.where(first, own[rows, :], d[rows, :]))
    out[MAIN + STRIP : MAIN + 2 * STRIP, :] = stay[STRIP:, :]
    out[MAIN + 2 * STRIP :, :] = back[STRIP:, :]


def slope(x):
    lane = lax.broadcasted_iota(jnp.int32, x.shape, 1)
    ahead = jnp.where(lane == SIZE - 1, 0.0, pltpu.roll(x, SIZE - 1, 1))
    behind = jnp.where(lane == 0, 0.0, pltpu.roll(x, 1, 1))
    return ahead - behind


def advance_kernel(ens, stay, back, own, d, c, b, a, got, out, shift, rims, lines, columns, pad, div, slope_u):
    step = pl.program_id(0)

    @pl.when(step == 0)
    def _():
        member, patch = here()
        core, z = patch % 2, (patch // 2) % 2
        first = core == 0
        for j, m in enumerate((a, b, c, d)):
            value = m[0:CHUNK, :]
            if j == 3:
                value = jnp.where(first, own[0:CHUNK, :], value)
            shift[pl.ds(pl.multiple_of(slot_chunk(member, core, j) * CHUNK, 8), CHUNK), :] = value
            at = pl.multiple_of(slot_chunk(member, core, j + 4) * CHUNK, 8)
            shift[pl.ds(at, CHUNK), :] = got[j * CHUNK : (j + 1) * CHUNK, :]
        for side in range(4):
            rows = slice(2 * CHUNK + side * USED, 2 * CHUNK + (side + 1) * USED)
            moved = (a[rows, :] + b[rows, :]) + (c[rows, :] + jnp.where(first, own[rows, :], d[rows, :]))
            moved = moved + got[MAIN + side * USED : MAIN + (side + 1) * USED, :]
            rows = slice(side * USED, (side + 1) * USED)
            for source, who in (
                (stay[rows, :], 2 * core + z),
                (back[rows, :], 2 * core + 1 - z),
                (got[MAIN + STRIP + side * USED : MAIN + STRIP + (side + 1) * USED, :], 2 - 2 * core + z),
                (got[MAIN + 2 * STRIP + side * USED : MAIN + 2 * STRIP + (side + 1) * USED, :], 3 - 2 * core - z),
            ):
                rims[who, side] = source + moved
        for n in range(LOCAL):
            at = n * 32
            lines[pl.ds(at, PLANES, stride=2), :] = rims[n, 3, 0:PLANES, :]
            lines[pl.ds(at + 1, PLANES, stride=2), :] = rims[n, 2, 0:PLANES, :]
            right = 0.5 * (rims[n, 3, PLANES:USED, :] + slope(rims[n, 3, LEV : 2 * LEV, :]))
            left = 0.5 * (slope(rims[n, 2, LEV : 2 * LEV, :]) - rims[n, 2, PLANES:USED, :])
            lines[pl.ds(at + 24, LEV, stride=2), :] = right
            lines[pl.ds(at + 25, LEV, stride=2), :] = left
        turned = lines[...].T
        for n in range(LOCAL):
            columns[n] = turned if n == 0 else pltpu.roll(turned, SIZE - 32 * n, 1)

    part = 32
    lane = lax.broadcasted_iota(jnp.int32, (part, SIZE), 1)
    at_left, at_right = lane == 0, lane == SIZE - 1

    def across(x, r, line):
        edge = pltpu.roll(columns[step, r : r + part, :], (SIZE - 1 - 2 * line) % SIZE, 1)
        return jnp.where(at_right, edge, pltpu.roll(x, SIZE - 1, 1)) - jnp.where(at_left, edge, pltpu.roll(x, 1, 1))

    for lev in range(LEV):
        for f in range(3):
            i = f * LEV + lev
            pad[f, 8 : 8 + SIZE, :] = ens[step, i] + shift[i * SIZE : (i + 1) * SIZE, :]
            pad[f, 7:8, :] = rims[step, 0, i : i + 1, :]
            pad[f, 8 + SIZE : 9 + SIZE, :] = rims[step, 1, i : i + 1, :]
        i = PLANES + lev
        div[7:8, :] = 0.5 * (slope(pad[0, 7:8, :]) + pad[1, 8:9, :] - rims[step, 0, i : i + 1, :])
        div[8 + SIZE : 9 + SIZE, :] = 0.5 * (
            slope(pad[0, 8 + SIZE : 9 + SIZE, :]) + rims[step, 1, i : i + 1, :] - pad[1, 7 + SIZE : 8 + SIZE, :]
        )
        for r in range(0, SIZE, part):
            at = 8 + r
            du = across(pad[0, at : at + part, :], r, lev)
            slope_u[r : r + part, :] = du
            div[at : at + part, :] = 0.5 * (du + pad[1, at + 1 : at + 1 + part, :] - pad[1, at - 1 : at - 1 + part, :])
        for r in range(0, SIZE, part):
            at = 8 + r
            now = slice(at, at + part)
            up, down = slice(at - 1, at - 1 + part), slice(at + 1, at + 1 + part)
            u, v, w = pad[0, now, :], pad[1, now, :], pad[2, now, :]
            edge = pltpu.roll(columns[step, r : r + part, :], (SIZE - 1 - 2 * (PLANES + lev)) % SIZE, 1)
            edge = edge + jnp.where(at_left, 0.5 * u, -0.5 * u)
            mid = div[now, :]
            grad_x = jnp.where(at_right, edge, pltpu.roll(mid, SIZE - 1, 1)) - jnp.where(at_left, edge, pltpu.roll(mid, 1, 1))
            grad_y = div[down, :] - div[up, :]
            new_u = u - 0.2 * (u * slope_u[r : r + part, :] + v * (pad[0, down, :] - pad[0, up, :]))
            new_v = v - 0.2 * (u * across(v, r, LEV + lev) + v * (pad[1, down, :] - pad[1, up, :]))
            new_w = w - 0.2 * (u * across(w, r, 2 * LEV + lev) + v * (pad[2, down, :] - pad[2, up, :]))
            out[0, lev, r : r + part, :] = new_u + 0.1 * grad_x
            out[0, LEV + lev, r : r + part, :] = new_v + 0.1 * grad_y
            out[0, 2 * LEV + lev, r : r + part, :] = new_w


def advance(ensemble, stay, back, received, own, got):
    return pl.pallas_call(
        advance_kernel,
        out_shape=jax.ShapeDtypeStruct((LOCAL, PLANES, SIZE, SIZE), F32),
        grid=(LOCAL,),
        in_specs=[vmem()] * 9,
        out_specs=pl.BlockSpec((1, PLANES, SIZE, SIZE), lambda n: (n, 0, 0, 0)),
        scratch_shapes=[
            pltpu.VMEM((ROWS, SIZE), F32),
            pltpu.VMEM((LOCAL, 4, USED, SIZE), F32),
            pltpu.VMEM((SIZE, SIZE), F32),
            pltpu.VMEM((LOCAL, SIZE, SIZE), F32),
            pltpu.VMEM((3, SIZE + 16, SIZE), F32),
            pltpu.VMEM((SIZE + 16, SIZE), F32),
            pltpu.VMEM((SIZE, SIZE), F32),
        ],
        compiler_params=limit(12),
        cost_estimate=pl.CostEstimate(flops=40_000_000, bytes_accessed=8_000_000, transcendentals=0),
        name="advance",
    )(*on(pltpu.VMEM, ensemble, stay, back, own, *received[::-1], got))


def on_device(ensemble, control, owner, neighbours, codes):
    shape = ensemble.shape
    ensemble = ensemble.reshape(LOCAL, PLANES, SIZE, SIZE)
    control = control.reshape(PLANES, SIZE, SIZE)
    table = jnp.concatenate([neighbours.reshape(-1), codes.reshape(-1)])

    keep, give, stay, leave = prepare(owner, ensemble, control)
    came = send(leave, lambda m, d: (m, d ^ 2))
    got = swap_cores(give)
    messages = small(pack_kernel, "pack", [2 * CHUNK] * 4, [keep, got])
    received = exchange(messages)
    got = swap_cores(small(split_kernel, "split", 2 * RECORD, [stay, came]))
    group = small(group_kernel, "group", 4 * RECORD, [stay, came, got])
    acc = small(add_kernel, "add", 2 * CHUNK, received + [messages[3]])
    stay, leave, half = pick(table, group, *over_x(group))
    back = send(leave, lambda m, d: (m, d ^ 2))
    reduced = small(
        reduce_kernel, "reduce", 2 * CHUNK + 2 * STRIP, [acc, swap_cores(acc), half, swap_cores(half)]
    )
    received = exchange([reduced] * 4)
    got = swap_cores(
        small(share_kernel, "share", MAIN + 3 * STRIP, [reduced, *received[::-1], stay, back])
    )
    out = advance(ensemble, stay, back, received, reduced, got)
    return out.reshape(shape)


def solution(mesh):
    spec = P("member", None, None, "domain", None)
    return jax.shard_map(
        on_device, mesh=mesh, in_specs=(spec, spec, P(), P(), P()), out_specs=spec, check_vma=False
    )
```

```python
import jax
import jax.numpy as jnp
from jax import lax
from jax.experimental import pallas as pl
from jax.experimental.pallas import tpu as pltpu
from jax.sharding import PartitionSpec as P

MESH = ("member", "domain")
N_MEMBER = 8
N_DOMAIN = 16
SIZE = 128
PLANES = 12
LEV = 4
LOCAL = 4
MEMBERS = 32
ROWS = PLANES * SIZE
CHUNK = ROWS // N_MEMBER
HALF = ROWS // 2
TAKEN = 20
SLOT = 32
RECORD = 4 * SLOT
USED = 16
STRIP = 4 * USED
STEPS = (2, 1, 3)
F32 = jnp.float32


def pairs(target):
    out = []
    for m in range(N_MEMBER):
        for d in range(N_DOMAIN):
            to = target(m, d)
            if to is not None:
                out.append((m * N_DOMAIN + d, to[0] * N_DOMAIN + to[1]))
    return out


def send(array, target):
    return lax.ppermute(array, MESH, pairs(target))


def swap_cores(array):
    return send(array, lambda m, d: (m, d ^ 1))


def over_y(arrays):
    return [send(array, lambda m, d, k=k: (m ^ k, d)) for k, array in zip(STEPS, arrays)]


def over_z_hi(array):
    return send(array, lambda m, d: (m ^ 4, d))


def over_x(array):
    return [send(array, lambda m, d, x=x: (m, d ^ (4 * x))) for x in (1, 2, 3)]


def vmem():
    return pl.BlockSpec(memory_space=pltpu.VMEM)


def hbm():
    return pl.BlockSpec(memory_space=pltpu.HBM)


def shaped(*rows):
    return [pltpu.VMEM((r, SIZE), F32) for r in rows]


def on(space, *arrays):
    return [pltpu.with_memory_space_constraint(x, space) for x in arrays]


def limit(mib):
    return pltpu.CompilerParams(vmem_limit_bytes=mib << 20)


def here():
    return lax.axis_index("member"), lax.axis_index("domain")


def prepare_kernel(owner_hbm, ens_hbm, ctl_hbm, keep, give, stay, leave, ens, ctl, part, tile, turned, lines, edge, owner, sems, osem):
    member, patch = here()
    z = (patch // 2) % 2
    table = pltpu.make_async_copy(owner_hbm, owner, osem)
    table.start()
    copies = []
    for i in range(PLANES):
        a = pltpu.make_async_copy(ens_hbm.at[:, i], ens.at[:, i], sems.at[0, i])
        b = pltpu.make_async_copy(ctl_hbm.at[i], ctl.at[i], sems.at[1, i])
        a.start()
        b.start()
        copies.append((a, b))
    table.wait()
    flag = jnp.where(owner[patch] == member, 1.0, 0.0).astype(F32)
    for i in range(PLANES):
        for c in copies[i]:
            c.wait()
        spots = [(a // 2, (a % 2) * PLANES + i) for a in range(LOCAL)] + [(0, 24 + i) if i < 8 else (1, 16 + i)]
        for r in range(0, SIZE, 32):
            rows = pl.ds(r, 32)
            group = lax.broadcasted_iota(jnp.int32, (32, SIZE), 1) // 4
            xs = [ens[a, i, rows, :] for a in range(LOCAL)]
            total = (xs[0] + xs[1]) + (xs[2] + xs[3])
            value = flag * ctl[i, rows, :] - total * (1.0 / MEMBERS)
            part[pl.ds(i * SIZE + r, 32), :] = value
            for t in (0, 1):
                acc = tile[t, rows, :]
                for (where, s), x in zip(spots, xs + [value]):
                    if where == t:
                        acc = jnp.where(group == s, pltpu.roll(x, (4 * s + 2) % SIZE, 1), acc)
                tile[t, rows, :] = acc
        for side, k, row in ((0, 0, 0), (0, 1, 1), (1, 0, SIZE - 1), (1, 1, SIZE - 2)):
            at = k * PLANES + i
            if at < TAKEN:
                for a in range(LOCAL):
                    lines[a, side, at : at + 1, :] = ens[a, i, row : row + 1, :]
                edge[side, at : at + 1, :] = part[i * SIZE + row : i * SIZE + row + 1, :]
    turned[0] = tile[0].T
    turned[1] = tile[1].T
    for side, k, q in ((2, 0, 2), (2, 1, 3), (3, 0, 1), (3, 1, 0)):
        count = 8 if k else PLANES
        at = k * PLANES
        for a in range(LOCAL):
            lines[a, side, at : at + count, :] = turned[a // 2, pl.ds((a % 2) * 48 + q, count, stride=4), :]
        edge[side, at : at + 8, :] = turned[0, pl.ds(96 + q, 8, stride=4), :]
        if k == 0:
            edge[side, 8:12, :] = turned[1, pl.ds(96 + q, 4, stride=4), :]
    for out, who in ((stay, z), (leave, 1 - z)):
        for c in (0, 1):
            for side in range(4):
                at = c * RECORD + side * SLOT
                out[at : at + TAKEN, :] = lines[2 * c + who, side, 0:TAKEN, :]
                out[at + 20 : at + 30, :] = edge[side, 10 * c : 10 * c + 10, :]
                out[at + 30 : at + 32, :] = jnp.zeros((2, SIZE), F32)
    mine = member // 4
    keep[...] = part[pl.ds(pl.multiple_of(mine * HALF, 8), HALF), :]
    give[...] = part[pl.ds(pl.multiple_of((1 - mine) * HALF, 8), HALF), :]


def prepare(owner, ensemble, control):
    return pl.pallas_call(
        prepare_kernel,
        out_shape=shaped(HALF, HALF, 2 * RECORD, 2 * RECORD),
        in_specs=[hbm()] * 3,
        out_specs=[vmem()] * 4,
        scratch_shapes=[
            pltpu.VMEM((LOCAL, PLANES, SIZE, SIZE), F32),
            pltpu.VMEM((PLANES, SIZE, SIZE), F32),
            pltpu.VMEM((ROWS, SIZE), F32),
            pltpu.VMEM((2, SIZE, SIZE), F32),
            pltpu.VMEM((2, SIZE, SIZE), F32),
            pltpu.VMEM((LOCAL, 4, 24, SIZE), F32),
            pltpu.VMEM((4, 24, SIZE), F32),
            pltpu.SMEM((N_DOMAIN,), jnp.int32),
            pltpu.SemaphoreType.DMA((2, PLANES)),
            pltpu.SemaphoreType.DMA,
        ],
        compiler_params=limit(12),
        cost_estimate=pl.CostEstimate(flops=2_000_000, bytes_accessed=5_000_000, transcendentals=0),
        name="prepare",
    )(*on(pltpu.HBM, owner, ensemble, control))


def small(kernel, name, rows, arrays):
    one = isinstance(rows, int)
    return pl.pallas_call(
        kernel,
        out_shape=shaped(rows)[0] if one else shaped(*rows),
        in_specs=[vmem()] * len(arrays),
        out_specs=vmem() if one else [vmem()] * len(rows),
        compiler_params=limit(4),
        name=name,
    )(*on(pltpu.VMEM, *arrays))


def halve_kernel(keep, came, own, *outs):
    member, _ = here()
    for step, out in zip((0,) + STEPS, (own,) + outs):
        rows = pl.ds(pl.multiple_of((member % 4 ^ step) * CHUNK, 8), CHUNK)
        out[...] = keep[rows, :] + came[rows, :]


def split_kernel(stay, came, out):
    _, patch = here()
    rows = pl.ds(pl.multiple_of((1 - patch % 2) * RECORD, 8), RECORD)
    out[0:RECORD, :] = stay[rows, :]
    out[RECORD:, :] = came[rows, :]


def group_kernel(stay, came, got, out):
    _, patch = here()
    rows = pl.ds(pl.multiple_of((patch % 2) * RECORD, 8), RECORD)
    out[0:RECORD, :] = stay[rows, :]
    out[RECORD : 2 * RECORD, :] = got[0:RECORD, :]
    out[2 * RECORD : 3 * RECORD, :] = came[rows, :]
    out[3 * RECORD :, :] = got[RECORD:, :]


def pick_kernel(table_hbm, g0, g1, g3, g2, stay, stay_sib, leave, half, half_sib, table, sem):
    _, patch = here()
    copy = pltpu.make_async_copy(table_hbm, table, sem)
    copy.start()
    copy.wait()
    for q in range(4):
        to, base, rows = ((stay, 0, SLOT), (stay_sib, 0, SLOT), (leave, 0, 24), (leave, STRIP, 24))[q]
        for side in range(4):
            spot = (patch ^ q) * 4 + side
            away = table[spot] ^ patch
            code = table[64 + spot]
            source = pl.ds(pl.multiple_of((away % 4) * RECORD + (code % 4) * SLOT, 8), rows)
            value = g0[source, :]
            for x, g in ((1, g1), (2, g2), (3, g3)):
                value = jnp.where(away // 4 == x, g[source, :], value)
            lane = lax.broadcasted_iota(jnp.int32, value.shape, 1)
            value = jnp.take_along_axis(value, jnp.where(code // 4 == 1, SIZE - 1 - lane, lane), axis=1)
            at, depth = base + side * USED, 16 if side < 2 else 12
            to[at : at + PLANES, :] = value[0:PLANES]
            to[at + PLANES : at + USED, :] = value[depth : depth + LEV]
            if q < 2:
                to_half = (half, half_sib)[q]
                to_half[at : at + 10, :] = value[20:30]
                to_half[at + 10 : at + USED, :] = jnp.zeros((6, SIZE), F32)


def pick(table, g0, g1, g2, g3):
    return pl.pallas_call(
        pick_kernel,
        out_shape=shaped(STRIP, STRIP, 2 * STRIP, STRIP, STRIP),
        in_specs=[hbm()] + [vmem()] * 4,
        out_specs=[vmem()] * 5,
        scratch_shapes=[pltpu.SMEM((128,), jnp.int32), pltpu.SemaphoreType.DMA],
        compiler_params=limit(4),
        name="pick",
    )(*on(pltpu.HBM, table), *on(pltpu.VMEM, g0, g1, g3, g2))


def add_kernel(a, b, c, own, half, came, out):
    _, patch = here()
    first = patch % 2 == 0
    out[0:CHUNK, :] = (a[...] + b[...]) + (c[...] + own[...])
    for side in range(4):
        at = side * USED
        mine, other = half[at : at + USED, :], came[at : at + USED, :]
        low, high = jnp.where(first, mine, other), jnp.where(first, other, mine)
        at, depth = CHUNK + side * USED, 6 if side < 2 else 2
        out[at : at + 10, :] = low[0:10]
        out[at + 10 : at + 12, :] = high[0:2]
        out[at + 12 : at + 16, :] = high[depth : depth + LEV]


def gather_kernel(own, c, b, a, out):
    member, _ = here()
    for step, m in zip((0,) + STEPS, (own, a, b, c)):
        out[pl.ds(pl.multiple_of((member % 4 ^ step) * CHUNK, 8), CHUNK), :] = m[0:CHUNK, :]
    rows = slice(CHUNK, CHUNK + STRIP)
    out[HALF:, :] = (a[rows, :] + b[rows, :]) + (c[rows, :] + own[rows, :])


def couple_kernel(stay, back, out):
    out[0:STRIP, :] = stay[...]
    out[STRIP:, :] = back[STRIP:, :]


def slope(x):
    lane = lax.broadcasted_iota(jnp.int32, x.shape, 1)
    ahead = jnp.where(lane == SIZE - 1, 0.0, pltpu.roll(x, SIZE - 1, 1))
    behind = jnp.where(lane == 0, 0.0, pltpu.roll(x, 1, 1))
    return ahead - behind


def advance_kernel(ens_hbm, stay, back, got, own, other, out, ens, sems, shift, rims, lines, columns, pad, div, slope_u):
    step = pl.program_id(0)

    @pl.when(step == 0)
    def _():
        for n in range(LOCAL):
            pltpu.make_async_copy(ens_hbm.at[n], ens.at[n], sems.at[n]).start()
        member, patch = here()
        core, z = patch % 2, (patch // 2) % 2
        mine = member // 4
        shift[pl.ds(pl.multiple_of(mine * HALF, 8), HALF), :] = own[0:HALF, :]
        shift[pl.ds(pl.multiple_of((1 - mine) * HALF, 8), HALF), :] = other[0:HALF, :]
        for side in range(4):
            rows = slice(HALF + side * USED, HALF + (side + 1) * USED)
            moved = own[rows, :] + other[rows, :]
            rows = slice(side * USED, (side + 1) * USED)
            for source, who in (
                (stay[rows, :], 2 * core + z),
                (back[rows, :], 2 * core + 1 - z),
                (got[rows, :], 2 - 2 * core + z),
                (got[STRIP + side * USED : STRIP + (side + 1) * USED, :], 3 - 2 * core - z),
            ):
                rims[who, side] = source + moved
        for n in range(LOCAL):
            at = n * 32
            lines[pl.ds(at, PLANES, stride=2), :] = rims[n, 3, 0:PLANES, :]
            lines[pl.ds(at + 1, PLANES, stride=2), :] = rims[n, 2, 0:PLANES, :]
            right = 0.5 * (rims[n, 3, PLANES:USED, :] + slope(rims[n, 3, LEV : 2 * LEV, :]))
            left = 0.5 * (slope(rims[n, 2, LEV : 2 * LEV, :]) - rims[n, 2, PLANES:USED, :])
            lines[pl.ds(at + 24, LEV, stride=2), :] = right
            lines[pl.ds(at + 25, LEV, stride=2), :] = left
        turned = lines[...].T
        for n in range(LOCAL):
            columns[n] = turned if n == 0 else pltpu.roll(turned, SIZE - 32 * n, 1)

    pltpu.make_async_copy(ens_hbm.at[step], ens.at[step], sems.at[step]).wait()
    part = 32
    lane = lax.broadcasted_iota(jnp.int32, (part, SIZE), 1)
    at_left, at_right = lane == 0, lane == SIZE - 1

    def across(x, r, line):
        edge = pltpu.roll(columns[step, r : r + part, :], (SIZE - 1 - 2 * line) % SIZE, 1)
        return jnp.where(at_right, edge, pltpu.roll(x, SIZE - 1, 1)) - jnp.where(at_left, edge, pltpu.roll(x, 1, 1))

    for lev in range(LEV):
        for f in range(3):
            i = f * LEV + lev
            pad[f, 8 : 8 + SIZE, :] = ens[step, i] + shift[i * SIZE : (i + 1) * SIZE, :]
            pad[f, 7:8, :] = rims[step, 0, i : i + 1, :]
            pad[f, 8 + SIZE : 9 + SIZE, :] = rims[step, 1, i : i + 1, :]
        i = PLANES + lev
        div[7:8, :] = 0.5 * (slope(pad[0, 7:8, :]) + pad[1, 8:9, :] - rims[step, 0, i : i + 1, :])
        div[8 + SIZE : 9 + SIZE, :] = 0.5 * (
            slope(pad[0, 8 + SIZE : 9 + SIZE, :]) + rims[step, 1, i : i + 1, :] - pad[1, 7 + SIZE : 8 + SIZE, :]
        )
        for r in range(0, SIZE, part):
            at = 8 + r
            du = across(pad[0, at : at + part, :], r, lev)
            slope_u[r : r + part, :] = du
            div[at : at + part, :] = 0.5 * (du + pad[1, at + 1 : at + 1 + part, :] - pad[1, at - 1 : at - 1 + part, :])
        for r in range(0, SIZE, part):
            at = 8 + r
            now = slice(at, at + part)
            up, down = slice(at - 1, at - 1 + part), slice(at + 1, at + 1 + part)
            u, v, w = pad[0, now, :], pad[1, now, :], pad[2, now, :]
            edge = pltpu.roll(columns[step, r : r + part, :], (SIZE - 1 - 2 * (PLANES + lev)) % SIZE, 1)
            edge = edge + jnp.where(at_left, 0.5 * u, -0.5 * u)
            mid = div[now, :]
            grad_x = jnp.where(at_right, edge, pltpu.roll(mid, SIZE - 1, 1)) - jnp.where(at_left, edge, pltpu.roll(mid, 1, 1))
            grad_y = div[down, :] - div[up, :]
            new_u = u - 0.2 * (u * slope_u[r : r + part, :] + v * (pad[0, down, :] - pad[0, up, :]))
            new_v = v - 0.2 * (u * across(v, r, LEV + lev) + v * (pad[1, down, :] - pad[1, up, :]))
            new_w = w - 0.2 * (u * across(w, r, 2 * LEV + lev) + v * (pad[2, down, :] - pad[2, up, :]))
            out[0, lev, r : r + part, :] = new_u + 0.1 * grad_x
            out[0, LEV + lev, r : r + part, :] = new_v + 0.1 * grad_y
            out[0, 2 * LEV + lev, r : r + part, :] = new_w


def advance(ensemble, *arrays):
    return pl.pallas_call(
        advance_kernel,
        out_shape=jax.ShapeDtypeStruct((LOCAL, PLANES, SIZE, SIZE), F32),
        grid=(LOCAL,),
        in_specs=[hbm()] + [vmem()] * len(arrays),
        out_specs=pl.BlockSpec((1, PLANES, SIZE, SIZE), lambda n: (n, 0, 0, 0)),
        scratch_shapes=[
            pltpu.VMEM((LOCAL, PLANES, SIZE, SIZE), F32),
            pltpu.SemaphoreType.DMA((LOCAL,)),
            pltpu.VMEM((ROWS, SIZE), F32),
            pltpu.VMEM((LOCAL, 4, USED, SIZE), F32),
            pltpu.VMEM((SIZE, SIZE), F32),
            pltpu.VMEM((LOCAL, SIZE, SIZE), F32),
            pltpu.VMEM((3, SIZE + 16, SIZE), F32),
            pltpu.VMEM((SIZE + 16, SIZE), F32),
            pltpu.VMEM((SIZE, SIZE), F32),
        ],
        compiler_params=limit(12),
        cost_estimate=pl.CostEstimate(flops=40_000_000, bytes_accessed=8_000_000, transcendentals=0),
        name="advance",
    )(*on(pltpu.HBM, ensemble), *on(pltpu.VMEM, *arrays))


def on_device(ensemble, control, owner, neighbours, codes):
    shape = ensemble.shape
    ensemble = ensemble.reshape(LOCAL, PLANES, SIZE, SIZE)
    control = control.reshape(PLANES, SIZE, SIZE)
    table = jnp.concatenate([neighbours.reshape(-1), codes.reshape(-1)])

    keep, give, stay, leave = prepare(owner, ensemble, control)
    strips = send(leave, lambda m, d: (m, d ^ 2))
    came = over_z_hi(give)
    halves = swap_cores(small(split_kernel, "split", 2 * RECORD, [stay, strips]))
    group = small(group_kernel, "group", 4 * RECORD, [stay, strips, halves])
    chunk, *chunks = small(halve_kernel, "halve", [CHUNK] * 4, [keep, came])
    chunks = over_y(chunks)
    stay, stay_sib, leave, half, half_sib = pick(table, group, *over_x(group))
    back = send(leave, lambda m, d: (m, d ^ 2))
    got = swap_cores(small(couple_kernel, "couple", 2 * STRIP, [stay_sib, back]))
    chunk = small(add_kernel, "add", CHUNK + STRIP, [*chunks, chunk, half, swap_cores(half_sib)])
    chunks = over_y([chunk] * 3)
    own = small(gather_kernel, "gather", HALF + STRIP, [chunk, *chunks[::-1]])
    own, got = lax.optimization_barrier((own, got))
    out = advance(ensemble, stay, back, got, own, over_z_hi(own))
    return out.reshape(shape)


def solution(mesh):
    spec = P("member", None, None, "domain", None)
    return jax.shard_map(
        on_device, mesh=mesh, in_specs=(spec, spec, P(), P(), P()), out_specs=spec, check_vma=False
    )
```

```python
import jax
import jax.numpy as jnp
from jax import lax
from jax.experimental import pallas as pl
from jax.experimental.pallas import tpu as pltpu
from jax.sharding import PartitionSpec as P

MESH = ("member", "domain")
N_MEMBER = 8
N_DOMAIN = 16
SIZE = 128
PLANES = 12
LEV = 4
LOCAL = 4
MEMBERS = 32
ROWS = PLANES * SIZE
CHUNK = ROWS // N_MEMBER
HALF = ROWS // 2
TAKEN = 20
SLOT = 32
RECORD = 4 * SLOT
USED = 16
STRIP = 4 * USED
STEPS = (2, 1, 3)
F32 = jnp.float32


def pairs(target):
    out = []
    for m in range(N_MEMBER):
        for d in range(N_DOMAIN):
            to = target(m, d)
            if to is not None:
                out.append((m * N_DOMAIN + d, to[0] * N_DOMAIN + to[1]))
    return out


def send(array, target):
    return lax.ppermute(array, MESH, pairs(target))


def swap_cores(array):
    return send(array, lambda m, d: (m, d ^ 1))


def over_y(arrays):
    return [send(array, lambda m, d, k=k: (m ^ k, d)) for k, array in zip(STEPS, arrays)]


def over_z_hi(array):
    return send(array, lambda m, d: (m ^ 4, d))


def over_x(array):
    return [send(array, lambda m, d, x=x: (m, d ^ (4 * x))) for x in (1, 2, 3)]


def vmem():
    return pl.BlockSpec(memory_space=pltpu.VMEM)


def hbm():
    return pl.BlockSpec(memory_space=pltpu.HBM)


def shaped(*rows):
    return [pltpu.VMEM((r, SIZE), F32) for r in rows]


def on(space, *arrays):
    return [pltpu.with_memory_space_constraint(x, space) for x in arrays]


def limit(mib):
    return pltpu.CompilerParams(vmem_limit_bytes=mib << 20)


def here():
    return lax.axis_index("member"), lax.axis_index("domain")


def prepare_kernel(owner_hbm, ens_hbm, ctl_hbm, keep, give0, give1, give2, stay, leave, ens, ctl, part, tile, turned, lines, edge, owner, sems, osem):
    member, patch = here()
    z = (patch // 2) % 2
    table = pltpu.make_async_copy(owner_hbm, owner, osem)
    table.start()
    copies = []
    for i in range(PLANES):
        a = pltpu.make_async_copy(ens_hbm.at[:, i], ens.at[:, i], sems.at[0, i])
        b = pltpu.make_async_copy(ctl_hbm.at[i], ctl.at[i], sems.at[1, i])
        a.start()
        b.start()
        copies.append((a, b))
    table.wait()
    flag = jnp.where(owner[patch] == member, 1.0, 0.0).astype(F32)
    for i in range(PLANES):
        for c in copies[i]:
            c.wait()
        spots = [(a // 2, (a % 2) * PLANES + i) for a in range(LOCAL)] + [(0, 24 + i) if i < 8 else (1, 16 + i)]
        for r in range(0, SIZE, 32):
            rows = pl.ds(r, 32)
            group = lax.broadcasted_iota(jnp.int32, (32, SIZE), 1) // 4
            xs = [ens[a, i, rows, :] for a in range(LOCAL)]
            total = (xs[0] + xs[1]) + (xs[2] + xs[3])
            value = flag * ctl[i, rows, :] - total * (1.0 / MEMBERS)
            part[pl.ds(i * SIZE + r, 32), :] = value
            for t in (0, 1):
                acc = tile[t, rows, :]
                for (where, s), x in zip(spots, xs + [value]):
                    if where == t:
                        acc = jnp.where(group == s, pltpu.roll(x, (4 * s + 2) % SIZE, 1), acc)
                tile[t, rows, :] = acc
        for side, k, row in ((0, 0, 0), (0, 1, 1), (1, 0, SIZE - 1), (1, 1, SIZE - 2)):
            at = k * PLANES + i
            if at < TAKEN:
                for a in range(LOCAL):
                    lines[a, side, at : at + 1, :] = ens[a, i, row : row + 1, :]
                edge[side, at : at + 1, :] = part[i * SIZE + row : i * SIZE + row + 1, :]
    turned[0] = tile[0].T
    turned[1] = tile[1].T
    for side, k, q in ((2, 0, 2), (2, 1, 3), (3, 0, 1), (3, 1, 0)):
        count = 8 if k else PLANES
        at = k * PLANES
        for a in range(LOCAL):
            lines[a, side, at : at + count, :] = turned[a // 2, pl.ds((a % 2) * 48 + q, count, stride=4), :]
        edge[side, at : at + 8, :] = turned[0, pl.ds(96 + q, 8, stride=4), :]
        if k == 0:
            edge[side, 8:12, :] = turned[1, pl.ds(96 + q, 4, stride=4), :]
    for out, who in ((stay, z), (leave, 1 - z)):
        for c in (0, 1):
            for side in range(4):
                at = c * RECORD + side * SLOT
                out[at : at + TAKEN, :] = lines[2 * c + who, side, 0:TAKEN, :]
                out[at + 20 : at + 30, :] = edge[side, 10 * c : 10 * c + 10, :]
                out[at + 30 : at + 32, :] = jnp.zeros((2, SIZE), F32)
    for step, out in zip((0,) + STEPS, (keep, give0, give1, give2)):
        for half in (0, 1):
            at = pl.multiple_of(half * HALF + (member % 4 ^ step) * CHUNK, 8)
            out[half * CHUNK : (half + 1) * CHUNK, :] = part[pl.ds(at, CHUNK), :]


def prepare(owner, ensemble, control):
    return pl.pallas_call(
        prepare_kernel,
        out_shape=shaped(*[2 * CHUNK] * 4, 2 * RECORD, 2 * RECORD),
        in_specs=[hbm()] * 3,
        out_specs=[vmem()] * 6,
        scratch_shapes=[
            pltpu.VMEM((LOCAL, PLANES, SIZE, SIZE), F32),
            pltpu.VMEM((PLANES, SIZE, SIZE), F32),
            pltpu.VMEM((ROWS, SIZE), F32),
            pltpu.VMEM((2, SIZE, SIZE), F32),
            pltpu.VMEM((2, SIZE, SIZE), F32),
            pltpu.VMEM((LOCAL, 4, 24, SIZE), F32),
            pltpu.VMEM((4, 24, SIZE), F32),
            pltpu.SMEM((N_DOMAIN,), jnp.int32),
            pltpu.SemaphoreType.DMA((2, PLANES)),
            pltpu.SemaphoreType.DMA,
        ],
        compiler_params=limit(12),
        cost_estimate=pl.CostEstimate(flops=2_000_000, bytes_accessed=5_000_000, transcendentals=0),
        name="prepare",
    )(*on(pltpu.HBM, owner, ensemble, control))


def small(kernel, name, rows, arrays):
    one = isinstance(rows, int)
    return pl.pallas_call(
        kernel,
        out_shape=shaped(rows)[0] if one else shaped(*rows),
        in_specs=[vmem()] * len(arrays),
        out_specs=vmem() if one else [vmem()] * len(rows),
        compiler_params=limit(4),
        name=name,
    )(*on(pltpu.VMEM, *arrays))


def sum_kernel(*refs):
    *terms, out = [r[...] for r in refs[:-1]] + [refs[-1]]
    while len(terms) > 1:
        terms = [terms[i] + terms[i + 1] if i + 1 < len(terms) else terms[i] for i in range(0, len(terms), 2)]
    out[...] = terms[0]


def split_kernel(stay, came, out):
    _, patch = here()
    rows = pl.ds(pl.multiple_of((1 - patch % 2) * RECORD, 8), RECORD)
    out[0:RECORD, :] = stay[rows, :]
    out[RECORD:, :] = came[rows, :]


def group_kernel(stay, came, got, out):
    _, patch = here()
    rows = pl.ds(pl.multiple_of((patch % 2) * RECORD, 8), RECORD)
    out[0:RECORD, :] = stay[rows, :]
    out[RECORD : 2 * RECORD, :] = got[0:RECORD, :]
    out[2 * RECORD : 3 * RECORD, :] = came[rows, :]
    out[3 * RECORD :, :] = got[RECORD:, :]


def pick_kernel(table_hbm, g0, g1, g3, g2, stay, stay_sib, leave, half, half_sib, table, sem):
    _, patch = here()
    copy = pltpu.make_async_copy(table_hbm, table, sem)
    copy.start()
    copy.wait()
    for q in range(4):
        to, base, rows = ((stay, 0, SLOT), (stay_sib, 0, SLOT), (leave, 0, 24), (leave, STRIP, 24))[q]
        for side in range(4):
            spot = (patch ^ q) * 4 + side
            away = table[spot] ^ patch
            code = table[64 + spot]
            source = pl.ds(pl.multiple_of((away % 4) * RECORD + (code % 4) * SLOT, 8), rows)
            value = g0[source, :]
            for x, g in ((1, g1), (2, g2), (3, g3)):
                value = jnp.where(away // 4 == x, g[source, :], value)
            lane = lax.broadcasted_iota(jnp.int32, value.shape, 1)
            value = jnp.take_along_axis(value, jnp.where(code // 4 == 1, SIZE - 1 - lane, lane), axis=1)
            at, depth = base + side * USED, 16 if side < 2 else 12
            to[at : at + PLANES, :] = value[0:PLANES]
            to[at + PLANES : at + USED, :] = value[depth : depth + LEV]
            if q < 2:
                to_half = (half, half_sib)[q]
                to_half[at : at + 10, :] = value[20:30]
                to_half[at + 10 : at + USED, :] = jnp.zeros((6, SIZE), F32)


def pick(table, g0, g1, g2, g3):
    return pl.pallas_call(
        pick_kernel,
        out_shape=shaped(STRIP, STRIP, 2 * STRIP, STRIP, STRIP),
        in_specs=[hbm()] + [vmem()] * 4,
        out_specs=[vmem()] * 5,
        scratch_shapes=[pltpu.SMEM((128,), jnp.int32), pltpu.SemaphoreType.DMA],
        compiler_params=limit(4),
        name="pick",
    )(*on(pltpu.HBM, table), *on(pltpu.VMEM, g0, g1, g3, g2))


def merge_kernel(half, came, out):
    _, patch = here()
    first = patch % 2 == 0
    for side in range(4):
        at = side * USED
        mine, other = half[at : at + USED, :], came[at : at + USED, :]
        low, high = jnp.where(first, mine, other), jnp.where(first, other, mine)
        depth = 6 if side < 2 else 2
        out[at : at + 10, :] = low[0:10]
        out[at + 10 : at + 12, :] = high[0:2]
        out[at + 12 : at + 16, :] = high[depth : depth + LEV]


def couple_kernel(stay, back, out):
    out[0:STRIP, :] = stay[...]
    out[STRIP:, :] = back[STRIP:, :]


def slope(x):
    lane = lax.broadcasted_iota(jnp.int32, x.shape, 1)
    ahead = jnp.where(lane == SIZE - 1, 0.0, pltpu.roll(x, SIZE - 1, 1))
    behind = jnp.where(lane == 0, 0.0, pltpu.roll(x, 1, 1))
    return ahead - behind


def advance_kernel(ens_hbm, stay, back, got, own, c, b, a, edge0, edge1, edge2, edge3, out, ens, sems, shift, rims, lines, columns, pad, div, slope_u):
    now_at = pl.program_id(0)

    @pl.when(now_at == 0)
    def _():
        for n in range(LOCAL):
            pltpu.make_async_copy(ens_hbm.at[n], ens.at[n], sems.at[n]).start()
        member, patch = here()
        core, z = patch % 2, (patch // 2) % 2
        for step, m in zip((0,) + STEPS, (own, a, b, c)):
            for half in (0, 1):
                at = pl.multiple_of(half * HALF + (member % 4 ^ step) * CHUNK, 8)
                shift[pl.ds(at, CHUNK), :] = m[half * CHUNK : (half + 1) * CHUNK, :]
        for side in range(4):
            rows = slice(side * USED, (side + 1) * USED)
            moved = (edge0[rows, :] + edge1[rows, :]) + (edge2[rows, :] + edge3[rows, :])
            for source, who in (
                (stay[rows, :], 2 * core + z),
                (back[rows, :], 2 * core + 1 - z),
                (got[rows, :], 2 - 2 * core + z),
                (got[STRIP + side * USED : STRIP + (side + 1) * USED, :], 3 - 2 * core - z),
            ):
                rims[who, side] = source + moved
        for n in range(LOCAL):
            at = n * 32
            lines[pl.ds(at, PLANES, stride=2), :] = rims[n, 3, 0:PLANES, :]
            lines[pl.ds(at + 1, PLANES, stride=2), :] = rims[n, 2, 0:PLANES, :]
            right = 0.5 * (rims[n, 3, PLANES:USED, :] + slope(rims[n, 3, LEV : 2 * LEV, :]))
            left = 0.5 * (slope(rims[n, 2, LEV : 2 * LEV, :]) - rims[n, 2, PLANES:USED, :])
            lines[pl.ds(at + 24, LEV, stride=2), :] = right
            lines[pl.ds(at + 25, LEV, stride=2), :] = left
        turned = lines[...].T
        for n in range(LOCAL):
            columns[n] = turned if n == 0 else pltpu.roll(turned, SIZE - 32 * n, 1)

    step = now_at
    pltpu.make_async_copy(ens_hbm.at[step], ens.at[step], sems.at[step]).wait()
    part = 32
    lane = lax.broadcasted_iota(jnp.int32, (part, SIZE), 1)
    at_left, at_right = lane == 0, lane == SIZE - 1

    def across(x, r, line):
        edge = pltpu.roll(columns[step, r : r + part, :], (SIZE - 1 - 2 * line) % SIZE, 1)
        return jnp.where(at_right, edge, pltpu.roll(x, SIZE - 1, 1)) - jnp.where(at_left, edge, pltpu.roll(x, 1, 1))

    for lev in range(LEV):
        for f in range(3):
            i = f * LEV + lev
            pad[f, 8 : 8 + SIZE, :] = ens[step, i] + shift[i * SIZE : (i + 1) * SIZE, :]
            pad[f, 7:8, :] = rims[step, 0, i : i + 1, :]
            pad[f, 8 + SIZE : 9 + SIZE, :] = rims[step, 1, i : i + 1, :]
        i = PLANES + lev
        div[7:8, :] = 0.5 * (slope(pad[0, 7:8, :]) + pad[1, 8:9, :] - rims[step, 0, i : i + 1, :])
        div[8 + SIZE : 9 + SIZE, :] = 0.5 * (
            slope(pad[0, 8 + SIZE : 9 + SIZE, :]) + rims[step, 1, i : i + 1, :] - pad[1, 7 + SIZE : 8 + SIZE, :]
        )
        for r in range(0, SIZE, part):
            at = 8 + r
            du = across(pad[0, at : at + part, :], r, lev)
            slope_u[r : r + part, :] = du
            div[at : at + part, :] = 0.5 * (du + pad[1, at + 1 : at + 1 + part, :] - pad[1, at - 1 : at - 1 + part, :])
        for r in range(0, SIZE, part):
            at = 8 + r
            now = slice(at, at + part)
            up, down = slice(at - 1, at - 1 + part), slice(at + 1, at + 1 + part)
            u, v, w = pad[0, now, :], pad[1, now, :], pad[2, now, :]
            edge = pltpu.roll(columns[step, r : r + part, :], (SIZE - 1 - 2 * (PLANES + lev)) % SIZE, 1)
            edge = edge + jnp.where(at_left, 0.5 * u, -0.5 * u)
            mid = div[now, :]
            grad_x = jnp.where(at_right, edge, pltpu.roll(mid, SIZE - 1, 1)) - jnp.where(at_left, edge, pltpu.roll(mid, 1, 1))
            grad_y = div[down, :] - div[up, :]
            new_u = u - 0.2 * (u * slope_u[r : r + part, :] + v * (pad[0, down, :] - pad[0, up, :]))
            new_v = v - 0.2 * (u * across(v, r, LEV + lev) + v * (pad[1, down, :] - pad[1, up, :]))
            new_w = w - 0.2 * (u * across(w, r, 2 * LEV + lev) + v * (pad[2, down, :] - pad[2, up, :]))
            out[0, lev, r : r + part, :] = new_u + 0.1 * grad_x
            out[0, LEV + lev, r : r + part, :] = new_v + 0.1 * grad_y
            out[0, 2 * LEV + lev, r : r + part, :] = new_w


def advance(ensemble, *arrays):
    return pl.pallas_call(
        advance_kernel,
        out_shape=jax.ShapeDtypeStruct((LOCAL, PLANES, SIZE, SIZE), F32),
        grid=(LOCAL,),
        in_specs=[hbm()] + [vmem()] * len(arrays),
        out_specs=pl.BlockSpec((1, PLANES, SIZE, SIZE), lambda n: (n, 0, 0, 0)),
        scratch_shapes=[
            pltpu.VMEM((LOCAL, PLANES, SIZE, SIZE), F32),
            pltpu.SemaphoreType.DMA((LOCAL,)),
            pltpu.VMEM((ROWS, SIZE), F32),
            pltpu.VMEM((LOCAL, 4, USED, SIZE), F32),
            pltpu.VMEM((SIZE, SIZE), F32),
            pltpu.VMEM((LOCAL, SIZE, SIZE), F32),
            pltpu.VMEM((3, SIZE + 16, SIZE), F32),
            pltpu.VMEM((SIZE + 16, SIZE), F32),
            pltpu.VMEM((SIZE, SIZE), F32),
        ],
        compiler_params=limit(12),
        cost_estimate=pl.CostEstimate(flops=40_000_000, bytes_accessed=8_000_000, transcendentals=0),
        name="advance",
    )(*on(pltpu.HBM, ensemble), *on(pltpu.VMEM, *arrays))


def on_device(ensemble, control, owner, neighbours, codes):
    shape = ensemble.shape
    ensemble = ensemble.reshape(LOCAL, PLANES, SIZE, SIZE)
    control = control.reshape(PLANES, SIZE, SIZE)
    table = jnp.concatenate([neighbours.reshape(-1), codes.reshape(-1)])

    keep, *gives, stay, leave = prepare(owner, ensemble, control)
    strips = send(leave, lambda m, d: (m, d ^ 2))
    halves = swap_cores(small(split_kernel, "split", 2 * RECORD, [stay, strips]))
    group = small(group_kernel, "group", 4 * RECORD, [stay, strips, halves])
    total = small(sum_kernel, "total", 2 * CHUNK, [*over_y(gives), keep])
    total = small(sum_kernel, "shift", 2 * CHUNK, [total, over_z_hi(total)])
    chunks = over_y([total] * 3)
    stay, stay_sib, leave, half, half_sib = pick(table, group, *over_x(group))
    back = send(leave, lambda m, d: (m, d ^ 2))
    got = swap_cores(small(couple_kernel, "couple", 2 * STRIP, [stay_sib, back]))
    edge = small(merge_kernel, "merge", STRIP, [half, swap_cores(half_sib)])
    edge = small(sum_kernel, "edge", STRIP, [edge, over_z_hi(edge)])
    edges = over_y([edge] * 3)
    out = advance(ensemble, stay, back, got, total, *chunks[::-1], edge, *edges[::-1])
    return out.reshape(shape)


def solution(mesh):
    spec = P("member", None, None, "domain", None)
    return jax.shard_map(
        on_device, mesh=mesh, in_specs=(spec, spec, P(), P(), P()), out_specs=spec, check_vma=False
    )
```

```python
import jax
import jax.numpy as jnp
from jax import lax
from jax.experimental import pallas as pl
from jax.experimental.pallas import tpu as pltpu
from jax.sharding import PartitionSpec as P

MESH = ("member", "domain")
N_MEMBER = 8
N_DOMAIN = 16
SIZE = 128
PLANES = 12
LEV = 4
LOCAL = 4
MEMBERS = 32
ROWS = PLANES * SIZE
CHUNK = ROWS // N_MEMBER
HALF = ROWS // 2
TAKEN = 20
SLOT = 32
RECORD = 4 * SLOT
USED = 16
STRIP = 4 * USED
STEPS = (1, 3, 2)
F32 = jnp.float32


def pairs(target):
    out = []
    for m in range(N_MEMBER):
        for d in range(N_DOMAIN):
            to = target(m, d)
            if to is not None:
                out.append((m * N_DOMAIN + d, to[0] * N_DOMAIN + to[1]))
    return out


def send(array, target):
    return lax.ppermute(array, MESH, pairs(target))


def swap_cores(array):
    return send(array, lambda m, d: (m, d ^ 1))


def over_y(arrays):
    return [send(array, lambda m, d, k=k: (m ^ k, d)) for k, array in zip(STEPS, arrays)]


def over_z_hi(array):
    return send(array, lambda m, d: (m ^ 4, d))


def over_x(array):
    return [send(array, lambda m, d, x=x: (m, d ^ (4 * x))) for x in (1, 2, 3)]


def vmem():
    return pl.BlockSpec(memory_space=pltpu.VMEM)


def hbm():
    return pl.BlockSpec(memory_space=pltpu.HBM)


def shaped(*rows):
    return [pltpu.VMEM((r, SIZE), F32) for r in rows]


def on(space, *arrays):
    return [pltpu.with_memory_space_constraint(x, space) for x in arrays]


def limit(mib):
    return pltpu.CompilerParams(vmem_limit_bytes=mib << 20)


def here():
    return lax.axis_index("member"), lax.axis_index("domain")


def prepare_kernel(owner_hbm, ens_hbm, ctl_hbm, keep, give0, give1, give2, stay, leave, ens, ctl, part, tile, turned, lines, edge, owner, sems, osem):
    member, patch = here()
    z = (patch // 2) % 2
    table = pltpu.make_async_copy(owner_hbm, owner, osem)
    table.start()
    copies = []
    for i in range(PLANES):
        a = pltpu.make_async_copy(ens_hbm.at[:, i], ens.at[:, i], sems.at[0, i])
        b = pltpu.make_async_copy(ctl_hbm.at[i], ctl.at[i], sems.at[1, i])
        a.start()
        b.start()
        copies.append((a, b))
    table.wait()
    flag = jnp.where(owner[patch] == member, 1.0, 0.0).astype(F32)
    for i in range(PLANES):
        for c in copies[i]:
            c.wait()
        spots = [(a // 2, (a % 2) * PLANES + i) for a in range(LOCAL)] + [(0, 24 + i) if i < 8 else (1, 16 + i)]
        for r in range(0, SIZE, 32):
            rows = pl.ds(r, 32)
            group = lax.broadcasted_iota(jnp.int32, (32, SIZE), 1) // 4
            xs = [ens[a, i, rows, :] for a in range(LOCAL)]
            total = (xs[0] + xs[1]) + (xs[2] + xs[3])
            value = flag * ctl[i, rows, :] - total * (1.0 / MEMBERS)
            part[pl.ds(i * SIZE + r, 32), :] = value
            for t in (0, 1):
                acc = tile[t, rows, :]
                for (where, s), x in zip(spots, xs + [value]):
                    if where == t:
                        acc = jnp.where(group == s, pltpu.roll(x, (4 * s + 2) % SIZE, 1), acc)
                tile[t, rows, :] = acc
        for side, k, row in ((0, 0, 0), (0, 1, 1), (1, 0, SIZE - 1), (1, 1, SIZE - 2)):
            at = k * PLANES + i
            if at < TAKEN:
                for a in range(LOCAL):
                    lines[a, side, at : at + 1, :] = ens[a, i, row : row + 1, :]
                edge[side, at : at + 1, :] = part[i * SIZE + row : i * SIZE + row + 1, :]
    turned[0] = tile[0].T
    turned[1] = tile[1].T
    for side, k, q in ((2, 0, 2), (2, 1, 3), (3, 0, 1), (3, 1, 0)):
        count = 8 if k else PLANES
        at = k * PLANES
        for a in range(LOCAL):
            lines[a, side, at : at + count, :] = turned[a // 2, pl.ds((a % 2) * 48 + q, count, stride=4), :]
        edge[side, at : at + 8, :] = turned[0, pl.ds(96 + q, 8, stride=4), :]
        if k == 0:
            edge[side, 8:12, :] = turned[1, pl.ds(96 + q, 4, stride=4), :]
    for out, who in ((stay, z), (leave, 1 - z)):
        for c in (0, 1):
            for side in range(4):
                at = c * RECORD + side * SLOT
                out[at : at + TAKEN, :] = lines[2 * c + who, side, 0:TAKEN, :]
                out[at + 20 : at + 30, :] = edge[side, 10 * c : 10 * c + 10, :]
                out[at + 30 : at + 32, :] = jnp.zeros((2, SIZE), F32)
    for step, out in zip((0,) + STEPS, (keep, give0, give1, give2)):
        for half in (0, 1):
            at = pl.multiple_of(half * HALF + (member % 4 ^ step) * CHUNK, 8)
            out[half * CHUNK : (half + 1) * CHUNK, :] = part[pl.ds(at, CHUNK), :]


def prepare(owner, ensemble, control):
    return pl.pallas_call(
        prepare_kernel,
        out_shape=shaped(*[2 * CHUNK] * 4, 2 * RECORD, 2 * RECORD),
        in_specs=[hbm()] * 3,
        out_specs=[vmem()] * 6,
        scratch_shapes=[
            pltpu.VMEM((LOCAL, PLANES, SIZE, SIZE), F32),
            pltpu.VMEM((PLANES, SIZE, SIZE), F32),
            pltpu.VMEM((ROWS, SIZE), F32),
            pltpu.VMEM((2, SIZE, SIZE), F32),
            pltpu.VMEM((2, SIZE, SIZE), F32),
            pltpu.VMEM((LOCAL, 4, 24, SIZE), F32),
            pltpu.VMEM((4, 24, SIZE), F32),
            pltpu.SMEM((N_DOMAIN,), jnp.int32),
            pltpu.SemaphoreType.DMA((2, PLANES)),
            pltpu.SemaphoreType.DMA,
        ],
        compiler_params=limit(12),
        cost_estimate=pl.CostEstimate(flops=2_000_000, bytes_accessed=5_000_000, transcendentals=0),
        name="prepare",
    )(*on(pltpu.HBM, owner, ensemble, control))


def small(kernel, name, rows, arrays):
    one = isinstance(rows, int)
    return pl.pallas_call(
        kernel,
        out_shape=shaped(rows)[0] if one else shaped(*rows),
        in_specs=[vmem()] * len(arrays),
        out_specs=vmem() if one else [vmem()] * len(rows),
        compiler_params=limit(4),
        name=name,
    )(*on(pltpu.VMEM, *arrays))


def sum_kernel(*refs):
    *terms, out = [r[...] for r in refs[:-1]] + [refs[-1]]
    while len(terms) > 1:
        terms = [terms[i] + terms[i + 1] if i + 1 < len(terms) else terms[i] for i in range(0, len(terms), 2)]
    out[...] = terms[0]


def split_kernel(stay, came, out):
    _, patch = here()
    rows = pl.ds(pl.multiple_of((1 - patch % 2) * RECORD, 8), RECORD)
    out[0:RECORD, :] = stay[rows, :]
    out[RECORD:, :] = came[rows, :]


def group_kernel(stay, came, got, out):
    _, patch = here()
    rows = pl.ds(pl.multiple_of((patch % 2) * RECORD, 8), RECORD)
    out[0:RECORD, :] = stay[rows, :]
    out[RECORD : 2 * RECORD, :] = got[0:RECORD, :]
    out[2 * RECORD : 3 * RECORD, :] = came[rows, :]
    out[3 * RECORD :, :] = got[RECORD:, :]


def pick_kernel(near_hbm, codes_hbm, g0, g1, g3, g2, stay, stay_sib, leave, half, half_sib, near, codes, sems):
    _, patch = here()
    copies = [
        pltpu.make_async_copy(near_hbm, near, sems.at[0]),
        pltpu.make_async_copy(codes_hbm, codes, sems.at[1]),
    ]
    for copy in copies:
        copy.start()
    for copy in copies:
        copy.wait()
    for q in range(4):
        to, base, rows = ((stay, 0, SLOT), (stay_sib, 0, SLOT), (leave, 0, 24), (leave, STRIP, 24))[q]
        for side in range(4):
            away = near[side, patch ^ q] ^ patch
            code = codes[side, patch ^ q]
            source = pl.ds(pl.multiple_of((away % 4) * RECORD + (code % 4) * SLOT, 8), rows)
            value = g0[source, :]
            for x, g in ((1, g1), (2, g2), (3, g3)):
                value = jnp.where(away // 4 == x, g[source, :], value)
            lane = lax.broadcasted_iota(jnp.int32, value.shape, 1)
            value = jnp.take_along_axis(value, jnp.where(code // 4 == 1, SIZE - 1 - lane, lane), axis=1)
            at, depth = base + side * USED, 16 if side < 2 else 12
            to[at : at + PLANES, :] = value[0:PLANES]
            to[at + PLANES : at + USED, :] = value[depth : depth + LEV]
            if q < 2:
                to_half = (half, half_sib)[q]
                to_half[at : at + 10, :] = value[20:30]
                to_half[at + 10 : at + USED, :] = jnp.zeros((6, SIZE), F32)


def pick(neighbours, codes, g0, g1, g2, g3):
    return pl.pallas_call(
        pick_kernel,
        out_shape=shaped(STRIP, STRIP, 2 * STRIP, STRIP, STRIP),
        in_specs=[hbm()] * 2 + [vmem()] * 4,
        out_specs=[vmem()] * 5,
        scratch_shapes=[pltpu.SMEM((4, N_DOMAIN), jnp.int32)] * 2 + [pltpu.SemaphoreType.DMA((2,))],
        compiler_params=limit(4),
        name="pick",
    )(*on(pltpu.HBM, neighbours, codes), *on(pltpu.VMEM, g0, g1, g3, g2))


def merge_kernel(half, came, out):
    _, patch = here()
    first = patch % 2 == 0
    for side in range(4):
        at = side * USED
        mine, other = half[at : at + USED, :], came[at : at + USED, :]
        low, high = jnp.where(first, mine, other), jnp.where(first, other, mine)
        depth = 6 if side < 2 else 2
        out[at : at + 10, :] = low[0:10]
        out[at + 10 : at + 12, :] = high[0:2]
        out[at + 12 : at + 16, :] = high[depth : depth + LEV]


def couple_kernel(stay, back, out):
    out[0:STRIP, :] = stay[...]
    out[STRIP:, :] = back[STRIP:, :]


def slope(x):
    lane = lax.broadcasted_iota(jnp.int32, x.shape, 1)
    ahead = jnp.where(lane == SIZE - 1, 0.0, pltpu.roll(x, SIZE - 1, 1))
    behind = jnp.where(lane == 0, 0.0, pltpu.roll(x, 1, 1))
    return ahead - behind


def recentre_kernel(ens_hbm, own, c, b, a, out, ens, shift, sems):
    copies = [pltpu.make_async_copy(ens_hbm.at[n], ens.at[n], sems.at[n]) for n in range(LOCAL)]
    for copy in copies:
        copy.start()
    member, _ = here()
    for step, m in zip((0,) + STEPS, (own, a, b, c)):
        for half in (0, 1):
            at = pl.multiple_of(half * HALF + (member % 4 ^ step) * CHUNK, 8)
            shift[pl.ds(at, CHUNK), :] = m[half * CHUNK : (half + 1) * CHUNK, :]
    for n in range(LOCAL):
        copies[n].wait()
        for i in range(PLANES):
            out[n, i, 0:8, :] = jnp.zeros((8, SIZE), F32)
            out[n, i, 8 + SIZE :, :] = jnp.zeros((8, SIZE), F32)
            for r in range(0, SIZE, 32):
                out[n, i, 8 + r : 40 + r, :] = ens[n, i, r : r + 32, :] + shift[i * SIZE + r : i * SIZE + r + 32, :]


def recentre(ensemble, arrays):
    return pl.pallas_call(
        recentre_kernel,
        out_shape=pltpu.VMEM((LOCAL, PLANES, SIZE + 16, SIZE), F32),
        in_specs=[hbm()] + [vmem()] * len(arrays),
        out_specs=vmem(),
        scratch_shapes=[
            pltpu.VMEM((LOCAL, PLANES, SIZE, SIZE), F32),
            pltpu.VMEM((ROWS, SIZE), F32),
            pltpu.SemaphoreType.DMA((LOCAL,)),
        ],
        compiler_params=limit(12),
        name="recentre",
    )(*on(pltpu.HBM, ensemble), *on(pltpu.VMEM, *arrays))


def advance_kernel(fields, stay, back, got, edge0, edge1, out, rims, lines, columns, div, slope_u):
    now_at = pl.program_id(0)

    @pl.when(now_at == 0)
    def _():
        _, patch = here()
        core, z = patch % 2, (patch // 2) % 2
        for side in range(4):
            rows = slice(side * USED, (side + 1) * USED)
            moved = edge0[rows, :] + edge1[rows, :]
            for source, who in (
                (stay[rows, :], 2 * core + z),
                (back[rows, :], 2 * core + 1 - z),
                (got[rows, :], 2 - 2 * core + z),
                (got[STRIP + side * USED : STRIP + (side + 1) * USED, :], 3 - 2 * core - z),
            ):
                rims[who, side] = source + moved
        for n in range(LOCAL):
            at = n * 32
            lines[pl.ds(at, PLANES, stride=2), :] = rims[n, 3, 0:PLANES, :]
            lines[pl.ds(at + 1, PLANES, stride=2), :] = rims[n, 2, 0:PLANES, :]
            right = 0.5 * (rims[n, 3, PLANES:USED, :] + slope(rims[n, 3, LEV : 2 * LEV, :]))
            left = 0.5 * (slope(rims[n, 2, LEV : 2 * LEV, :]) - rims[n, 2, PLANES:USED, :])
            lines[pl.ds(at + 24, LEV, stride=2), :] = right
            lines[pl.ds(at + 25, LEV, stride=2), :] = left
        turned = lines[...].T
        for n in range(LOCAL):
            columns[n] = turned if n == 0 else pltpu.roll(turned, SIZE - 32 * n, 1)

    step = now_at
    part = 32
    lane = lax.broadcasted_iota(jnp.int32, (part, SIZE), 1)
    row = lax.broadcasted_iota(jnp.int32, (part, SIZE), 0)
    at_left, at_right = lane == 0, lane == SIZE - 1

    def rows_at(i, r):
        return fields[step, i, 8 + r : 8 + r + part, :]

    def above(i, r):
        value = fields[step, i, 7 + r : 7 + r + part, :]
        return jnp.where(row == 0, rims[step, 0, i : i + 1, :], value) if r == 0 else value

    def below(i, r):
        value = fields[step, i, 9 + r : 9 + r + part, :]
        return jnp.where(row == part - 1, rims[step, 1, i : i + 1, :], value) if r == SIZE - part else value

    def across(x, r, line):
        edge = pltpu.roll(columns[step, r : r + part, :], (SIZE - 1 - 2 * line) % SIZE, 1)
        return jnp.where(at_right, edge, pltpu.roll(x, SIZE - 1, 1)) - jnp.where(at_left, edge, pltpu.roll(x, 1, 1))

    for lev in range(LEV):
        iu, iv, iw, deep = lev, LEV + lev, 2 * LEV + lev, PLANES + lev
        div[7:8, :] = 0.5 * (
            slope(rims[step, 0, iu : iu + 1, :]) + fields[step, iv, 8:9, :] - rims[step, 0, deep : deep + 1, :]
        )
        div[8 + SIZE : 9 + SIZE, :] = 0.5 * (
            slope(rims[step, 1, iu : iu + 1, :])
            + rims[step, 1, deep : deep + 1, :]
            - fields[step, iv, 7 + SIZE : 8 + SIZE, :]
        )
        for r in range(0, SIZE, part):
            du = across(rows_at(iu, r), r, iu)
            slope_u[r : r + part, :] = du
            div[8 + r : 8 + r + part, :] = 0.5 * (du + below(iv, r) - above(iv, r))
        for r in range(0, SIZE, part):
            u, v, w = rows_at(iu, r), rows_at(iv, r), rows_at(iw, r)
            edge = pltpu.roll(columns[step, r : r + part, :], (SIZE - 1 - 2 * deep) % SIZE, 1)
            edge = edge + jnp.where(at_left, 0.5 * u, -0.5 * u)
            mid = div[8 + r : 8 + r + part, :]
            grad_x = jnp.where(at_right, edge, pltpu.roll(mid, SIZE - 1, 1)) - jnp.where(at_left, edge, pltpu.roll(mid, 1, 1))
            grad_y = div[9 + r : 9 + r + part, :] - div[7 + r : 7 + r + part, :]
            new_u = u - 0.2 * (u * slope_u[r : r + part, :] + v * (below(iu, r) - above(iu, r)))
            new_v = v - 0.2 * (u * across(v, r, iv) + v * (below(iv, r) - above(iv, r)))
            new_w = w - 0.2 * (u * across(w, r, iw) + v * (below(iw, r) - above(iw, r)))
            out[0, iu, r : r + part, :] = new_u + 0.1 * grad_x
            out[0, iv, r : r + part, :] = new_v + 0.1 * grad_y
            out[0, iw, r : r + part, :] = new_w


def advance(*arrays):
    return pl.pallas_call(
        advance_kernel,
        out_shape=jax.ShapeDtypeStruct((LOCAL, PLANES, SIZE, SIZE), F32),
        grid=(LOCAL,),
        in_specs=[vmem()] * len(arrays),
        out_specs=pl.BlockSpec((1, PLANES, SIZE, SIZE), lambda n: (n, 0, 0, 0)),
        scratch_shapes=[
            pltpu.VMEM((LOCAL, 4, USED, SIZE), F32),
            pltpu.VMEM((SIZE, SIZE), F32),
            pltpu.VMEM((LOCAL, SIZE, SIZE), F32),
            pltpu.VMEM((SIZE + 16, SIZE), F32),
            pltpu.VMEM((SIZE, SIZE), F32),
        ],
        compiler_params=limit(8),
        cost_estimate=pl.CostEstimate(flops=40_000_000, bytes_accessed=8_000_000, transcendentals=0),
        name="advance",
    )(*on(pltpu.VMEM, *arrays))


def on_device(ensemble, control, owner, neighbours, codes):
    shape = ensemble.shape
    ensemble = ensemble.reshape(LOCAL, PLANES, SIZE, SIZE)
    control = control.reshape(PLANES, SIZE, SIZE)

    keep, *gives, stay, leave = prepare(owner, ensemble, control)
    strips = send(leave, lambda m, d: (m, d ^ 2))
    halves = swap_cores(small(split_kernel, "split", 2 * RECORD, [stay, strips]))
    group = small(group_kernel, "group", 4 * RECORD, [stay, strips, halves])
    total = small(sum_kernel, "total", 2 * CHUNK, [*over_y(gives), keep])
    total = small(sum_kernel, "shift", 2 * CHUNK, [total, over_z_hi(total)])
    chunks = over_y([total] * 3)
    stay, stay_sib, leave, half, half_sib = pick(neighbours.T, codes.T, group, *over_x(group))
    came = swap_cores(half_sib)
    back = send(leave, lambda m, d: (m, d ^ 2))
    got = swap_cores(small(couple_kernel, "couple", 2 * STRIP, [stay_sib, back]))
    edge = small(merge_kernel, "merge", STRIP, [half, came])
    edge = small(sum_kernel, "edge", STRIP, [edge, over_z_hi(edge)])
    edge = small(sum_kernel, "edge", STRIP, [edge, send(edge, lambda m, d: (m ^ 1, d))])
    other = send(edge, lambda m, d: (m ^ 3, d))
    fields = recentre(ensemble, [total, *chunks[::-1]])
    out = advance(fields, stay, back, got, edge, other)
    return out.reshape(shape)


def solution(mesh):
    spec = P("member", None, None, "domain", None)
    return jax.shard_map(
        on_device, mesh=mesh, in_specs=(spec, spec, P(), P(), P()), out_specs=spec, check_vma=False
    )
```

```python
import jax
import jax.numpy as jnp
from jax import lax
from jax.experimental import pallas as pl
from jax.experimental.pallas import tpu as pltpu
from jax.sharding import PartitionSpec as P

MESH = ("member", "domain")
N_MEMBER = 8
N_DOMAIN = 16
SIZE = 128
PLANES = 12
LEV = 4
LOCAL = 4
MEMBERS = 32
ROWS = PLANES * SIZE
CHUNK = ROWS // N_MEMBER
HALF = ROWS // 2
TAKEN = 20
SLOT = 32
RECORD = 4 * SLOT
USED = 16
STRIP = 4 * USED
STEPS = (1, 3, 2)
F32 = jnp.float32


def pairs(target):
    out = []
    for m in range(N_MEMBER):
        for d in range(N_DOMAIN):
            to = target(m, d)
            if to is not None:
                out.append((m * N_DOMAIN + d, to[0] * N_DOMAIN + to[1]))
    return out


def send(array, target):
    return lax.ppermute(array, MESH, pairs(target))


def swap_cores(array):
    return send(array, lambda m, d: (m, d ^ 1))


def over_y(arrays):
    return [send(array, lambda m, d, k=k: (m ^ k, d)) for k, array in zip(STEPS, arrays)]


def over_z_hi(array):
    return send(array, lambda m, d: (m ^ 4, d))


def over_x(array):
    return [send(array, lambda m, d, x=x: (m, d ^ (4 * x))) for x in (1, 2, 3)]


def vmem():
    return pl.BlockSpec(memory_space=pltpu.VMEM)


def hbm():
    return pl.BlockSpec(memory_space=pltpu.HBM)


def shaped(*rows):
    return [pltpu.VMEM((r, SIZE), F32) for r in rows]


def on(space, *arrays):
    return [pltpu.with_memory_space_constraint(x, space) for x in arrays]


def limit(mib):
    return pltpu.CompilerParams(vmem_limit_bytes=mib << 20)


def here():
    return lax.axis_index("member"), lax.axis_index("domain")


def prepare_kernel(owner_hbm, ens_hbm, ctl_hbm, keep, give0, give1, give2, stay, leave, ens, ctl, part, tile, turned, lines, edge, owner, sems, osem):
    member, patch = here()
    z = (patch // 2) % 2
    table = pltpu.make_async_copy(owner_hbm, owner, osem)
    table.start()
    copies = []
    for i in range(PLANES):
        a = pltpu.make_async_copy(ens_hbm.at[:, i], ens.at[:, i], sems.at[0, i])
        b = pltpu.make_async_copy(ctl_hbm.at[i], ctl.at[i], sems.at[1, i])
        a.start()
        b.start()
        copies.append((a, b))
    table.wait()
    flag = jnp.where(owner[patch] == member, 1.0, 0.0).astype(F32)
    for i in range(PLANES):
        for c in copies[i]:
            c.wait()
        spots = [(a // 2, (a % 2) * PLANES + i) for a in range(LOCAL)] + [(0, 24 + i) if i < 8 else (1, 16 + i)]
        for r in range(0, SIZE, 32):
            rows = pl.ds(r, 32)
            group = lax.broadcasted_iota(jnp.int32, (32, SIZE), 1) // 4
            xs = [ens[a, i, rows, :] for a in range(LOCAL)]
            total = (xs[0] + xs[1]) + (xs[2] + xs[3])
            value = flag * ctl[i, rows, :] - total * (1.0 / MEMBERS)
            part[pl.ds(i * SIZE + r, 32), :] = value
            for t in (0, 1):
                acc = tile[t, rows, :]
                for (where, s), x in zip(spots, xs + [value]):
                    if where == t:
                        acc = jnp.where(group == s, pltpu.roll(x, (4 * s + 2) % SIZE, 1), acc)
                tile[t, rows, :] = acc
        for side, k, row in ((0, 0, 0), (0, 1, 1), (1, 0, SIZE - 1), (1, 1, SIZE - 2)):
            at = k * PLANES + i
            if at < TAKEN:
                for a in range(LOCAL):
                    lines[a, side, at : at + 1, :] = ens[a, i, row : row + 1, :]
                edge[side, at : at + 1, :] = part[i * SIZE + row : i * SIZE + row + 1, :]
    turned[0] = tile[0].T
    turned[1] = tile[1].T
    for side, k, q in ((2, 0, 2), (2, 1, 3), (3, 0, 1), (3, 1, 0)):
        count = 8 if k else PLANES
        at = k * PLANES
        for a in range(LOCAL):
            lines[a, side, at : at + count, :] = turned[a // 2, pl.ds((a % 2) * 48 + q, count, stride=4), :]
        edge[side, at : at + 8, :] = turned[0, pl.ds(96 + q, 8, stride=4), :]
        if k == 0:
            edge[side, 8:12, :] = turned[1, pl.ds(96 + q, 4, stride=4), :]
    for out, who in ((stay, z), (leave, 1 - z)):
        for c in (0, 1):
            for side in range(4):
                at = c * RECORD + side * SLOT
                out[at : at + TAKEN, :] = lines[2 * c + who, side, 0:TAKEN, :]
                out[at + 20 : at + 30, :] = edge[side, 10 * c : 10 * c + 10, :]
                out[at + 30 : at + 32, :] = jnp.zeros((2, SIZE), F32)
    for step, out in zip((0,) + STEPS, (keep, give0, give1, give2)):
        for half in (0, 1):
            at = pl.multiple_of(half * HALF + (member % 4 ^ step) * CHUNK, 8)
            out[half * CHUNK : (half + 1) * CHUNK, :] = part[pl.ds(at, CHUNK), :]


def prepare(owner, ensemble, control):
    return pl.pallas_call(
        prepare_kernel,
        out_shape=shaped(*[2 * CHUNK] * 4, 2 * RECORD, 2 * RECORD),
        in_specs=[hbm()] * 3,
        out_specs=[vmem()] * 6,
        scratch_shapes=[
            pltpu.VMEM((LOCAL, PLANES, SIZE, SIZE), F32),
            pltpu.VMEM((PLANES, SIZE, SIZE), F32),
            pltpu.VMEM((ROWS, SIZE), F32),
            pltpu.VMEM((2, SIZE, SIZE), F32),
            pltpu.VMEM((2, SIZE, SIZE), F32),
            pltpu.VMEM((LOCAL, 4, 24, SIZE), F32),
            pltpu.VMEM((4, 24, SIZE), F32),
            pltpu.SMEM((N_DOMAIN,), jnp.int32),
            pltpu.SemaphoreType.DMA((2, PLANES)),
            pltpu.SemaphoreType.DMA,
        ],
        compiler_params=limit(12),
        cost_estimate=pl.CostEstimate(flops=2_000_000, bytes_accessed=5_000_000, transcendentals=0),
        name="prepare",
    )(*on(pltpu.HBM, owner, ensemble, control))


def small(kernel, name, rows, arrays):
    one = isinstance(rows, int)
    return pl.pallas_call(
        kernel,
        out_shape=shaped(rows)[0] if one else shaped(*rows),
        in_specs=[vmem()] * len(arrays),
        out_specs=vmem() if one else [vmem()] * len(rows),
        compiler_params=limit(4),
        name=name,
    )(*on(pltpu.VMEM, *arrays))


def sum_kernel(*refs):
    *terms, out = [r[...] for r in refs[:-1]] + [refs[-1]]
    while len(terms) > 1:
        terms = [terms[i] + terms[i + 1] if i + 1 < len(terms) else terms[i] for i in range(0, len(terms), 2)]
    out[...] = terms[0]


def split_kernel(stay, came, out):
    _, patch = here()
    rows = pl.ds(pl.multiple_of((1 - patch % 2) * RECORD, 8), RECORD)
    out[0:RECORD, :] = stay[rows, :]
    out[RECORD:, :] = came[rows, :]


def group_kernel(stay, came, got, out):
    _, patch = here()
    rows = pl.ds(pl.multiple_of((patch % 2) * RECORD, 8), RECORD)
    out[0:RECORD, :] = stay[rows, :]
    out[RECORD : 2 * RECORD, :] = got[0:RECORD, :]
    out[2 * RECORD : 3 * RECORD, :] = came[rows, :]
    out[3 * RECORD :, :] = got[RECORD:, :]


def pick_kernel(near_hbm, codes_hbm, g0, g1, g3, g2, stay, stay_sib, leave, half, half_sib, near, codes, sems):
    _, patch = here()
    copies = [
        pltpu.make_async_copy(near_hbm, near, sems.at[0]),
        pltpu.make_async_copy(codes_hbm, codes, sems.at[1]),
    ]
    for copy in copies:
        copy.start()
    for copy in copies:
        copy.wait()
    for q in range(4):
        to, base, rows = ((stay, 0, SLOT), (stay_sib, 0, SLOT), (leave, 0, 24), (leave, STRIP, 24))[q]
        for side in range(4):
            away = near[side, patch ^ q] ^ patch
            code = codes[side, patch ^ q]
            source = pl.ds(pl.multiple_of((away % 4) * RECORD + (code % 4) * SLOT, 8), rows)
            value = g0[source, :]
            for x, g in ((1, g1), (2, g2), (3, g3)):
                value = jnp.where(away // 4 == x, g[source, :], value)
            lane = lax.broadcasted_iota(jnp.int32, value.shape, 1)
            value = jnp.take_along_axis(value, jnp.where(code // 4 == 1, SIZE - 1 - lane, lane), axis=1)
            at, depth = base + side * USED, 16 if side < 2 else 12
            to[at : at + PLANES, :] = value[0:PLANES]
            to[at + PLANES : at + USED, :] = value[depth : depth + LEV]
            if q < 2:
                to_half = (half, half_sib)[q]
                to_half[at : at + 10, :] = value[20:30]
                to_half[at + 10 : at + USED, :] = jnp.zeros((6, SIZE), F32)


def pick(neighbours, codes, g0, g1, g2, g3):
    return pl.pallas_call(
        pick_kernel,
        out_shape=shaped(STRIP, STRIP, 2 * STRIP, STRIP, STRIP),
        in_specs=[hbm()] * 2 + [vmem()] * 4,
        out_specs=[vmem()] * 5,
        scratch_shapes=[pltpu.SMEM((4, N_DOMAIN), jnp.int32)] * 2 + [pltpu.SemaphoreType.DMA((2,))],
        compiler_params=limit(4),
        name="pick",
    )(*on(pltpu.HBM, neighbours, codes), *on(pltpu.VMEM, g0, g1, g3, g2))


def merge_kernel(half, came, out):
    _, patch = here()
    first = patch % 2 == 0
    for side in range(4):
        at = side * USED
        mine, other = half[at : at + USED, :], came[at : at + USED, :]
        low, high = jnp.where(first, mine, other), jnp.where(first, other, mine)
        depth = 6 if side < 2 else 2
        out[at : at + 10, :] = low[0:10]
        out[at + 10 : at + 12, :] = high[0:2]
        out[at + 12 : at + 16, :] = high[depth : depth + LEV]


def couple_kernel(stay, back, out):
    out[0:STRIP, :] = stay[...]
    out[STRIP:, :] = back[STRIP:, :]


def slope(x):
    lane = lax.broadcasted_iota(jnp.int32, x.shape, 1)
    ahead = jnp.where(lane == SIZE - 1, 0.0, pltpu.roll(x, SIZE - 1, 1))
    behind = jnp.where(lane == 0, 0.0, pltpu.roll(x, 1, 1))
    return ahead - behind


def recentre_kernel(ens_hbm, own, c, b, a, out, slopes, ens, shift, sems):
    copies = [pltpu.make_async_copy(ens_hbm.at[n], ens.at[n], sems.at[n]) for n in range(LOCAL)]
    for copy in copies:
        copy.start()
    member, _ = here()
    for step, m in zip((0,) + STEPS, (own, a, b, c)):
        for half in (0, 1):
            at = pl.multiple_of(half * HALF + (member % 4 ^ step) * CHUNK, 8)
            shift[pl.ds(at, CHUNK), :] = m[half * CHUNK : (half + 1) * CHUNK, :]
    for n in range(LOCAL):
        copies[n].wait()
        for i in range(PLANES):
            out[n, i, 0:8, :] = jnp.zeros((8, SIZE), F32)
            out[n, i, 8 + SIZE :, :] = jnp.zeros((8, SIZE), F32)
            for r in range(0, SIZE, 32):
                value = ens[n, i, r : r + 32, :] + shift[i * SIZE + r : i * SIZE + r + 32, :]
                out[n, i, 8 + r : 40 + r, :] = value
                slopes[n, i, r : r + 32, :] = slope(value)


def recentre(ensemble, arrays):
    return pl.pallas_call(
        recentre_kernel,
        out_shape=[
            pltpu.VMEM((LOCAL, PLANES, SIZE + 16, SIZE), F32),
            pltpu.VMEM((LOCAL, PLANES, SIZE, SIZE), F32),
        ],
        in_specs=[hbm()] + [vmem()] * len(arrays),
        out_specs=[vmem()] * 2,
        scratch_shapes=[
            pltpu.VMEM((LOCAL, PLANES, SIZE, SIZE), F32),
            pltpu.VMEM((ROWS, SIZE), F32),
            pltpu.SemaphoreType.DMA((LOCAL,)),
        ],
        compiler_params=limit(12),
        name="recentre",
    )(*on(pltpu.HBM, ensemble), *on(pltpu.VMEM, *arrays))


def advance_kernel(fields, slopes, stay, back, got, edge0, edge1, out, rims, lines, columns, div):
    now_at = pl.program_id(0)

    @pl.when(now_at == 0)
    def _():
        _, patch = here()
        core, z = patch % 2, (patch // 2) % 2
        for side in range(4):
            rows = slice(side * USED, (side + 1) * USED)
            moved = edge0[rows, :] + edge1[rows, :]
            for source, who in (
                (stay[rows, :], 2 * core + z),
                (back[rows, :], 2 * core + 1 - z),
                (got[rows, :], 2 - 2 * core + z),
                (got[STRIP + side * USED : STRIP + (side + 1) * USED, :], 3 - 2 * core - z),
            ):
                rims[who, side] = source + moved
        for n in range(LOCAL):
            at = n * 32
            lines[pl.ds(at, PLANES, stride=2), :] = rims[n, 3, 0:PLANES, :]
            lines[pl.ds(at + 1, PLANES, stride=2), :] = -rims[n, 2, 0:PLANES, :]
            right = 0.5 * (rims[n, 3, PLANES:USED, :] + slope(rims[n, 3, LEV : 2 * LEV, :]))
            left = 0.5 * (slope(rims[n, 2, LEV : 2 * LEV, :]) - rims[n, 2, PLANES:USED, :])
            lines[pl.ds(at + 24, LEV, stride=2), :] = right
            lines[pl.ds(at + 25, LEV, stride=2), :] = left
        turned = lines[...].T
        for n in range(LOCAL):
            columns[n] = turned if n == 0 else pltpu.roll(turned, SIZE - 32 * n, 1)

    step = now_at
    part = 32
    lane = lax.broadcasted_iota(jnp.int32, (part, SIZE), 1)
    row = lax.broadcasted_iota(jnp.int32, (part, SIZE), 0)
    at_left, at_right = lane == 0, lane == SIZE - 1

    def rows_at(i, r):
        return fields[step, i, 8 + r : 8 + r + part, :]

    def above(i, r):
        value = fields[step, i, 7 + r : 7 + r + part, :]
        return jnp.where(row == 0, rims[step, 0, i : i + 1, :], value) if r == 0 else value

    def below(i, r):
        value = fields[step, i, 9 + r : 9 + r + part, :]
        return jnp.where(row == part - 1, rims[step, 1, i : i + 1, :], value) if r == SIZE - part else value

    at_end = jnp.logical_or(at_left, at_right)

    def across(i, r):
        edge = pltpu.roll(columns[step, r : r + part, :], (SIZE - 1 - 2 * i) % SIZE, 1)
        return slopes[step, i, r : r + part, :] + jnp.where(at_end, edge, 0.0)

    for lev in range(LEV):
        iu, iv, iw, deep = lev, LEV + lev, 2 * LEV + lev, PLANES + lev
        div[7:8, :] = 0.5 * (
            slope(rims[step, 0, iu : iu + 1, :]) + fields[step, iv, 8:9, :] - rims[step, 0, deep : deep + 1, :]
        )
        div[8 + SIZE : 9 + SIZE, :] = 0.5 * (
            slope(rims[step, 1, iu : iu + 1, :])
            + rims[step, 1, deep : deep + 1, :]
            - fields[step, iv, 7 + SIZE : 8 + SIZE, :]
        )
        for r in range(0, SIZE, part):
            div[8 + r : 8 + r + part, :] = 0.5 * (across(iu, r) + below(iv, r) - above(iv, r))
        for r in range(0, SIZE, part):
            u, v, w = rows_at(iu, r), rows_at(iv, r), rows_at(iw, r)
            edge = pltpu.roll(columns[step, r : r + part, :], (SIZE - 1 - 2 * deep) % SIZE, 1)
            edge = edge + jnp.where(at_left, 0.5 * u, -0.5 * u)
            mid = div[8 + r : 8 + r + part, :]
            grad_x = jnp.where(at_right, edge, pltpu.roll(mid, SIZE - 1, 1)) - jnp.where(at_left, edge, pltpu.roll(mid, 1, 1))
            grad_y = div[9 + r : 9 + r + part, :] - div[7 + r : 7 + r + part, :]
            new_u = u - 0.2 * (u * across(iu, r) + v * (below(iu, r) - above(iu, r)))
            new_v = v - 0.2 * (u * across(iv, r) + v * (below(iv, r) - above(iv, r)))
            new_w = w - 0.2 * (u * across(iw, r) + v * (below(iw, r) - above(iw, r)))
            out[0, iu, r : r + part, :] = new_u + 0.1 * grad_x
            out[0, iv, r : r + part, :] = new_v + 0.1 * grad_y
            out[0, iw, r : r + part, :] = new_w


def advance(*arrays):
    return pl.pallas_call(
        advance_kernel,
        out_shape=jax.ShapeDtypeStruct((LOCAL, PLANES, SIZE, SIZE), F32),
        grid=(LOCAL,),
        in_specs=[vmem()] * len(arrays),
        out_specs=pl.BlockSpec((1, PLANES, SIZE, SIZE), lambda n: (n, 0, 0, 0)),
        scratch_shapes=[
            pltpu.VMEM((LOCAL, 4, USED, SIZE), F32),
            pltpu.VMEM((SIZE, SIZE), F32),
            pltpu.VMEM((LOCAL, SIZE, SIZE), F32),
            pltpu.VMEM((SIZE + 16, SIZE), F32),
        ],
        compiler_params=limit(8),
        cost_estimate=pl.CostEstimate(flops=40_000_000, bytes_accessed=8_000_000, transcendentals=0),
        name="advance",
    )(*on(pltpu.VMEM, *arrays))


def on_device(ensemble, control, owner, neighbours, codes):
    shape = ensemble.shape
    ensemble = ensemble.reshape(LOCAL, PLANES, SIZE, SIZE)
    control = control.reshape(PLANES, SIZE, SIZE)

    keep, *gives, stay, leave = prepare(owner, ensemble, control)
    strips = send(leave, lambda m, d: (m, d ^ 2))
    halves = swap_cores(small(split_kernel, "split", 2 * RECORD, [stay, strips]))
    group = small(group_kernel, "group", 4 * RECORD, [stay, strips, halves])
    total = small(sum_kernel, "total", 2 * CHUNK, [*over_y(gives), keep])
    total = small(sum_kernel, "shift", 2 * CHUNK, [total, over_z_hi(total)])
    chunks = over_y([total] * 3)
    stay, stay_sib, leave, half, half_sib = pick(neighbours.T, codes.T, group, *over_x(group))
    came = swap_cores(half_sib)
    back = send(leave, lambda m, d: (m, d ^ 2))
    got = swap_cores(small(couple_kernel, "couple", 2 * STRIP, [stay_sib, back]))
    edge = small(merge_kernel, "merge", STRIP, [half, came])
    edge = small(sum_kernel, "edge", STRIP, [edge, over_z_hi(edge)])
    edge = small(sum_kernel, "edge", STRIP, [edge, send(edge, lambda m, d: (m ^ 1, d))])
    other = send(edge, lambda m, d: (m ^ 3, d))
    fields, slopes = recentre(ensemble, [total, *chunks[::-1]])
    out = advance(fields, slopes, stay, back, got, edge, other)
    return out.reshape(shape)


def solution(mesh):
    spec = P("member", None, None, "domain", None)
    return jax.shard_map(
        on_device, mesh=mesh, in_specs=(spec, spec, P(), P(), P()), out_specs=spec, check_vma=False
    )
```

```python
import jax
import jax.numpy as jnp
from jax import lax
from jax.experimental import pallas as pl
from jax.experimental.pallas import tpu as pltpu
from jax.sharding import PartitionSpec as P

MESH = ("member", "domain")
N_MEMBER = 8
N_DOMAIN = 16
SIZE = 128
PLANES = 12
LEV = 4
LOCAL = 4
MEMBERS = 32
ROWS = PLANES * SIZE
CHUNK = ROWS // N_MEMBER
HALF = ROWS // 2
TAKEN = 20
SLOT = 32
RECORD = 4 * SLOT
USED = 16
STRIP = 4 * USED
STEPS = (1, 3, 2)
F32 = jnp.float32


def pairs(target):
    out = []
    for m in range(N_MEMBER):
        for d in range(N_DOMAIN):
            to = target(m, d)
            if to is not None:
                out.append((m * N_DOMAIN + d, to[0] * N_DOMAIN + to[1]))
    return out


def send(array, target):
    return lax.ppermute(array, MESH, pairs(target))


def swap_cores(array):
    return send(array, lambda m, d: (m, d ^ 1))


def over_y(arrays):
    return [send(array, lambda m, d, k=k: (m ^ k, d)) for k, array in zip(STEPS, arrays)]


def over_z_hi(array):
    return send(array, lambda m, d: (m ^ 4, d))


def over_x(array):
    return [send(array, lambda m, d, x=x: (m, d ^ (4 * x))) for x in (1, 2, 3)]


def vmem():
    return pl.BlockSpec(memory_space=pltpu.VMEM)


def hbm():
    return pl.BlockSpec(memory_space=pltpu.HBM)


def shaped(*rows):
    return [pltpu.VMEM((r, SIZE), F32) for r in rows]


def on(space, *arrays):
    return [pltpu.with_memory_space_constraint(x, space) for x in arrays]


def limit(mib):
    return pltpu.CompilerParams(vmem_limit_bytes=mib << 20)


def here():
    return lax.axis_index("member"), lax.axis_index("domain")


def prepare_kernel(owner_hbm, ens_hbm, ctl_hbm, keep, give0, give1, give2, stay, leave, ens, ctl, part, tile, turned, lines, edge, owner, sems, osem):
    member, patch = here()
    z = (patch // 2) % 2
    table = pltpu.make_async_copy(owner_hbm, owner, osem)
    table.start()
    copies = []
    for i in range(PLANES):
        a = pltpu.make_async_copy(ens_hbm.at[:, i], ens.at[:, i], sems.at[0, i])
        b = pltpu.make_async_copy(ctl_hbm.at[i], ctl.at[i], sems.at[1, i])
        a.start()
        b.start()
        copies.append((a, b))
    table.wait()
    flag = jnp.where(owner[patch] == member, 1.0, 0.0).astype(F32)
    for i in range(PLANES):
        for c in copies[i]:
            c.wait()
        spots = [(a // 2, (a % 2) * PLANES + i) for a in range(LOCAL)] + [(0, 24 + i) if i < 8 else (1, 16 + i)]
        for r in range(0, SIZE, 32):
            rows = pl.ds(r, 32)
            group = lax.broadcasted_iota(jnp.int32, (32, SIZE), 1) // 4
            xs = [ens[a, i, rows, :] for a in range(LOCAL)]
            total = (xs[0] + xs[1]) + (xs[2] + xs[3])
            value = flag * ctl[i, rows, :] - total * (1.0 / MEMBERS)
            part[pl.ds(i * SIZE + r, 32), :] = value
            for t in (0, 1):
                acc = tile[t, rows, :]
                for (where, s), x in zip(spots, xs + [value]):
                    if where == t:
                        acc = jnp.where(group == s, pltpu.roll(x, (4 * s + 2) % SIZE, 1), acc)
                tile[t, rows, :] = acc
        for side, k, row in ((0, 0, 0), (0, 1, 1), (1, 0, SIZE - 1), (1, 1, SIZE - 2)):
            at = k * PLANES + i
            if at < TAKEN:
                for a in range(LOCAL):
                    lines[a, side, at : at + 1, :] = ens[a, i, row : row + 1, :]
                edge[side, at : at + 1, :] = part[i * SIZE + row : i * SIZE + row + 1, :]
    turned[0] = tile[0].T
    turned[1] = tile[1].T
    for side, k, q in ((2, 0, 2), (2, 1, 3), (3, 0, 1), (3, 1, 0)):
        count = 8 if k else PLANES
        at = k * PLANES
        for a in range(LOCAL):
            lines[a, side, at : at + count, :] = turned[a // 2, pl.ds((a % 2) * 48 + q, count, stride=4), :]
        edge[side, at : at + 8, :] = turned[0, pl.ds(96 + q, 8, stride=4), :]
        if k == 0:
            edge[side, 8:12, :] = turned[1, pl.ds(96 + q, 4, stride=4), :]
    for out, who in ((stay, z), (leave, 1 - z)):
        for c in (0, 1):
            for side in range(4):
                at = c * RECORD + side * SLOT
                out[at : at + TAKEN, :] = lines[2 * c + who, side, 0:TAKEN, :]
                out[at + 20 : at + 30, :] = edge[side, 10 * c : 10 * c + 10, :]
                out[at + 30 : at + 32, :] = jnp.zeros((2, SIZE), F32)
    for step, out in zip((0,) + STEPS, (keep, give0, give1, give2)):
        for half in (0, 1):
            at = pl.multiple_of(half * HALF + (member % 4 ^ step) * CHUNK, 8)
            out[half * CHUNK : (half + 1) * CHUNK, :] = part[pl.ds(at, CHUNK), :]


def prepare(owner, ensemble, control):
    return pl.pallas_call(
        prepare_kernel,
        out_shape=shaped(*[2 * CHUNK] * 4, 2 * RECORD, 2 * RECORD),
        in_specs=[hbm()] * 3,
        out_specs=[vmem()] * 6,
        scratch_shapes=[
            pltpu.VMEM((LOCAL, PLANES, SIZE, SIZE), F32),
            pltpu.VMEM((PLANES, SIZE, SIZE), F32),
            pltpu.VMEM((ROWS, SIZE), F32),
            pltpu.VMEM((2, SIZE, SIZE), F32),
            pltpu.VMEM((2, SIZE, SIZE), F32),
            pltpu.VMEM((LOCAL, 4, 24, SIZE), F32),
            pltpu.VMEM((4, 24, SIZE), F32),
            pltpu.SMEM((N_DOMAIN,), jnp.int32),
            pltpu.SemaphoreType.DMA((2, PLANES)),
            pltpu.SemaphoreType.DMA,
        ],
        compiler_params=limit(12),
        cost_estimate=pl.CostEstimate(flops=2_000_000, bytes_accessed=5_000_000, transcendentals=0),
        name="prepare",
    )(*on(pltpu.HBM, owner, ensemble, control))


def small(kernel, name, rows, arrays):
    one = isinstance(rows, int)
    return pl.pallas_call(
        kernel,
        out_shape=shaped(rows)[0] if one else shaped(*rows),
        in_specs=[vmem()] * len(arrays),
        out_specs=vmem() if one else [vmem()] * len(rows),
        compiler_params=limit(4),
        name=name,
    )(*on(pltpu.VMEM, *arrays))


def sum_kernel(*refs):
    *terms, out = [r[...] for r in refs[:-1]] + [refs[-1]]
    while len(terms) > 1:
        terms = [terms[i] + terms[i + 1] if i + 1 < len(terms) else terms[i] for i in range(0, len(terms), 2)]
    out[...] = terms[0]


def split_kernel(stay, came, out):
    _, patch = here()
    rows = pl.ds(pl.multiple_of((1 - patch % 2) * RECORD, 8), RECORD)
    out[0:RECORD, :] = stay[rows, :]
    out[RECORD:, :] = came[rows, :]


def group_kernel(stay, came, got, out):
    _, patch = here()
    rows = pl.ds(pl.multiple_of((patch % 2) * RECORD, 8), RECORD)
    out[0:RECORD, :] = stay[rows, :]
    out[RECORD : 2 * RECORD, :] = got[0:RECORD, :]
    out[2 * RECORD : 3 * RECORD, :] = came[rows, :]
    out[3 * RECORD :, :] = got[RECORD:, :]


def pick_kernel(near_hbm, codes_hbm, g0, g1, g3, g2, stay, stay_sib, leave, half, half_sib, near, codes, sems):
    _, patch = here()
    copies = [
        pltpu.make_async_copy(near_hbm, near, sems.at[0]),
        pltpu.make_async_copy(codes_hbm, codes, sems.at[1]),
    ]
    for copy in copies:
        copy.start()
    for copy in copies:
        copy.wait()
    for q in range(4):
        to, base, rows = ((stay, 0, SLOT), (stay_sib, 0, SLOT), (leave, 0, 24), (leave, STRIP, 24))[q]
        for side in range(4):
            away = near[side, patch ^ q] ^ patch
            code = codes[side, patch ^ q]
            source = pl.ds(pl.multiple_of((away % 4) * RECORD + (code % 4) * SLOT, 8), rows)
            value = g0[source, :]
            for x, g in ((1, g1), (2, g2), (3, g3)):
                value = jnp.where(away // 4 == x, g[source, :], value)
            lane = lax.broadcasted_iota(jnp.int32, value.shape, 1)
            value = jnp.take_along_axis(value, jnp.where(code // 4 == 1, SIZE - 1 - lane, lane), axis=1)
            at, depth = base + side * USED, 16 if side < 2 else 12
            to[at : at + PLANES, :] = value[0:PLANES]
            to[at + PLANES : at + USED, :] = value[depth : depth + LEV]
            if q < 2:
                to_half = (half, half_sib)[q]
                to_half[at : at + 10, :] = value[20:30]
                to_half[at + 10 : at + USED, :] = jnp.zeros((6, SIZE), F32)


def pick(neighbours, codes, g0, g1, g2, g3):
    return pl.pallas_call(
        pick_kernel,
        out_shape=shaped(STRIP, STRIP, 2 * STRIP, STRIP, STRIP),
        in_specs=[hbm()] * 2 + [vmem()] * 4,
        out_specs=[vmem()] * 5,
        scratch_shapes=[pltpu.SMEM((4, N_DOMAIN), jnp.int32)] * 2 + [pltpu.SemaphoreType.DMA((2,))],
        compiler_params=limit(4),
        name="pick",
    )(*on(pltpu.HBM, neighbours, codes), *on(pltpu.VMEM, g0, g1, g3, g2))


def merge_kernel(half, came, out):
    _, patch = here()
    first = patch % 2 == 0
    for side in range(4):
        at = side * USED
        mine, other = half[at : at + USED, :], came[at : at + USED, :]
        low, high = jnp.where(first, mine, other), jnp.where(first, other, mine)
        depth = 6 if side < 2 else 2
        out[at : at + 10, :] = low[0:10]
        out[at + 10 : at + 12, :] = high[0:2]
        out[at + 12 : at + 16, :] = high[depth : depth + LEV]


def couple_kernel(stay, back, out):
    out[0:STRIP, :] = stay[...]
    out[STRIP:, :] = back[STRIP:, :]


def slope(x):
    lane = lax.broadcasted_iota(jnp.int32, x.shape, 1)
    ahead = jnp.where(lane == SIZE - 1, 0.0, pltpu.roll(x, SIZE - 1, 1))
    behind = jnp.where(lane == 0, 0.0, pltpu.roll(x, 1, 1))
    return ahead - behind


def recentre_kernel(ens_hbm, own, c, b, a, out, slopes, ens, shift, sems):
    copies = [pltpu.make_async_copy(ens_hbm.at[n], ens.at[n], sems.at[n]) for n in range(LOCAL)]
    for copy in copies:
        copy.start()
    member, _ = here()
    for step, m in zip((0,) + STEPS, (own, a, b, c)):
        for half in (0, 1):
            at = pl.multiple_of(half * HALF + (member % 4 ^ step) * CHUNK, 8)
            shift[pl.ds(at, CHUNK), :] = m[half * CHUNK : (half + 1) * CHUNK, :]
    for n in range(LOCAL):
        copies[n].wait()
        for i in range(PLANES):
            out[n, i, 0:8, :] = jnp.zeros((8, SIZE), F32)
            out[n, i, 8 + SIZE :, :] = jnp.zeros((8, SIZE), F32)
            for r in range(0, SIZE, 32):
                value = ens[n, i, r : r + 32, :] + shift[i * SIZE + r : i * SIZE + r + 32, :]
                out[n, i, 8 + r : 40 + r, :] = value
                slopes[n, i, r : r + 32, :] = slope(value)


def recentre(ensemble, arrays):
    return pl.pallas_call(
        recentre_kernel,
        out_shape=[
            pltpu.VMEM((LOCAL, PLANES, SIZE + 16, SIZE), F32),
            pltpu.VMEM((LOCAL, PLANES, SIZE, SIZE), F32),
        ],
        in_specs=[hbm()] + [vmem()] * len(arrays),
        out_specs=[vmem()] * 2,
        scratch_shapes=[
            pltpu.VMEM((LOCAL, PLANES, SIZE, SIZE), F32),
            pltpu.VMEM((ROWS, SIZE), F32),
            pltpu.SemaphoreType.DMA((LOCAL,)),
        ],
        compiler_params=limit(12),
        name="recentre",
    )(*on(pltpu.HBM, ensemble), *on(pltpu.VMEM, *arrays))


def advance_kernel(fields, slopes, stay, back, got, edge0, edge1, out, rims, lines, columns, div):
    now_at = pl.program_id(0)

    @pl.when(now_at == 0)
    def _():
        _, patch = here()
        core, z = patch % 2, (patch // 2) % 2
        for side in range(4):
            rows = slice(side * USED, (side + 1) * USED)
            moved = edge0[rows, :] + edge1[rows, :]
            for source, who in (
                (stay[rows, :], 2 * core + z),
                (back[rows, :], 2 * core + 1 - z),
                (got[rows, :], 2 - 2 * core + z),
                (got[STRIP + side * USED : STRIP + (side + 1) * USED, :], 3 - 2 * core - z),
            ):
                rims[who, side] = source + moved
        for n in range(LOCAL):
            at = n * 32
            lines[pl.ds(at, PLANES, stride=2), :] = rims[n, 3, 0:PLANES, :]
            lines[pl.ds(at + 1, PLANES, stride=2), :] = -rims[n, 2, 0:PLANES, :]
            right = 0.5 * (rims[n, 3, PLANES:USED, :] + slope(rims[n, 3, LEV : 2 * LEV, :]))
            left = 0.5 * (slope(rims[n, 2, LEV : 2 * LEV, :]) - rims[n, 2, PLANES:USED, :])
            lines[pl.ds(at + 24, LEV, stride=2), :] = right
            lines[pl.ds(at + 25, LEV, stride=2), :] = left
        turned = lines[...].T
        for n in range(LOCAL):
            columns[n] = turned if n == 0 else pltpu.roll(turned, SIZE - 32 * n, 1)

    step = now_at
    part = 32
    lane = lax.broadcasted_iota(jnp.int32, (part, SIZE), 1)
    row = lax.broadcasted_iota(jnp.int32, (part, SIZE), 0)
    at_left, at_right = lane == 0, lane == SIZE - 1

    def rows_at(i, r):
        return fields[step, i, 8 + r : 8 + r + part, :]

    def above(i, r):
        value = fields[step, i, 7 + r : 7 + r + part, :]
        return jnp.where(row == 0, rims[step, 0, i : i + 1, :], value) if r == 0 else value

    def below(i, r):
        value = fields[step, i, 9 + r : 9 + r + part, :]
        return jnp.where(row == part - 1, rims[step, 1, i : i + 1, :], value) if r == SIZE - part else value

    at_end = jnp.logical_or(at_left, at_right)

    def across(i, r):
        edge = pltpu.roll(columns[step, r : r + part, :], (SIZE - 1 - 2 * i) % SIZE, 1)
        return slopes[step, i, r : r + part, :] + jnp.where(at_end, edge, 0.0)

    for lev in range(LEV):
        iu, iv, iw, deep = lev, LEV + lev, 2 * LEV + lev, PLANES + lev
        div[7:8, :] = 0.5 * (
            slope(rims[step, 0, iu : iu + 1, :]) + fields[step, iv, 8:9, :] - rims[step, 0, deep : deep + 1, :]
        )
        div[8 + SIZE : 9 + SIZE, :] = 0.5 * (
            slope(rims[step, 1, iu : iu + 1, :])
            + rims[step, 1, deep : deep + 1, :]
            - fields[step, iv, 7 + SIZE : 8 + SIZE, :]
        )
        for r in range(0, SIZE, part):
            div[8 + r : 8 + r + part, :] = 0.5 * (across(iu, r) + below(iv, r) - above(iv, r))
        for r in range(0, SIZE, part):
            u, v, w = rows_at(iu, r), rows_at(iv, r), rows_at(iw, r)
            edge = pltpu.roll(columns[step, r : r + part, :], (SIZE - 1 - 2 * deep) % SIZE, 1)
            edge = edge + jnp.where(at_left, 0.5 * u, -0.5 * u)
            mid = div[8 + r : 8 + r + part, :]
            grad_x = jnp.where(at_right, edge, pltpu.roll(mid, SIZE - 1, 1)) - jnp.where(at_left, edge, pltpu.roll(mid, 1, 1))
            grad_y = div[9 + r : 9 + r + part, :] - div[7 + r : 7 + r + part, :]
            new_u = u - 0.2 * (u * across(iu, r) + v * (below(iu, r) - above(iu, r)))
            new_v = v - 0.2 * (u * across(iv, r) + v * (below(iv, r) - above(iv, r)))
            new_w = w - 0.2 * (u * across(iw, r) + v * (below(iw, r) - above(iw, r)))
            out[0, iu, r : r + part, :] = new_u + 0.1 * grad_x
            out[0, iv, r : r + part, :] = new_v + 0.1 * grad_y
            out[0, iw, r : r + part, :] = new_w


def advance(*arrays):
    return pl.pallas_call(
        advance_kernel,
        out_shape=jax.ShapeDtypeStruct((LOCAL, PLANES, SIZE, SIZE), F32),
        grid=(LOCAL,),
        in_specs=[vmem()] * len(arrays),
        out_specs=pl.BlockSpec((1, PLANES, SIZE, SIZE), lambda n: (n, 0, 0, 0)),
        scratch_shapes=[
            pltpu.VMEM((LOCAL, 4, USED, SIZE), F32),
            pltpu.VMEM((SIZE, SIZE), F32),
            pltpu.VMEM((LOCAL, SIZE, SIZE), F32),
            pltpu.VMEM((SIZE + 16, SIZE), F32),
        ],
        compiler_params=limit(8),
        cost_estimate=pl.CostEstimate(flops=40_000_000, bytes_accessed=8_000_000, transcendentals=0),
        name="advance",
    )(*on(pltpu.VMEM, *arrays))


def on_device(ensemble, control, owner, neighbours, codes):
    shape = ensemble.shape
    ensemble = ensemble.reshape(LOCAL, PLANES, SIZE, SIZE)
    control = control.reshape(PLANES, SIZE, SIZE)

    keep, *gives, stay, leave = prepare(owner, ensemble, control)
    strips = send(leave, lambda m, d: (m, d ^ 2))
    halves = swap_cores(small(split_kernel, "split", 2 * RECORD, [stay, strips]))
    group = small(group_kernel, "group", 4 * RECORD, [stay, strips, halves])
    total = small(sum_kernel, "total", 2 * CHUNK, [*over_y(gives), keep])
    total = small(sum_kernel, "shift", 2 * CHUNK, [total, over_z_hi(total)])
    chunks = over_y([total] * 3)
    stay, stay_sib, leave, half, half_sib = pick(neighbours.T, codes.T, group, *over_x(group))
    came = swap_cores(half_sib)
    back = send(leave, lambda m, d: (m, d ^ 2))
    got = swap_cores(small(couple_kernel, "couple", 2 * STRIP, [stay_sib, back]))
    edge = small(merge_kernel, "merge", STRIP, [half, came])
    edge = small(sum_kernel, "edge", STRIP, [edge, send(edge, lambda m, d: (m ^ 1, d))])
    edge = small(sum_kernel, "edge", STRIP, [edge, send(edge, lambda m, d: (m ^ 3, d))])
    other = over_z_hi(edge)
    fields, slopes = recentre(ensemble, [total, *chunks[::-1]])
    out = advance(fields, slopes, stay, back, got, edge, other)
    return out.reshape(shape)


def solution(mesh):
    spec = P("member", None, None, "domain", None)
    return jax.shard_map(
        on_device, mesh=mesh, in_specs=(spec, spec, P(), P(), P()), out_specs=spec, check_vma=False
    )
```

```python
import jax
import jax.numpy as jnp
from jax import lax
from jax.experimental import pallas as pl
from jax.experimental.pallas import tpu as pltpu
from jax.sharding import PartitionSpec as P

MESH = ("member", "domain")
N_MEMBER = 8
N_DOMAIN = 16
SIZE = 128
PLANES = 12
LEV = 4
LOCAL = 4
MEMBERS = 32
ROWS = PLANES * SIZE
CHUNK = ROWS // N_MEMBER
HALF = ROWS // 2
TAKEN = 20
SLOT = 32
RECORD = 4 * SLOT
USED = 16
STRIP = 4 * USED
STEPS = (1, 3, 2)
F32 = jnp.float32


def pairs(target):
    out = []
    for m in range(N_MEMBER):
        for d in range(N_DOMAIN):
            to = target(m, d)
            if to is not None:
                out.append((m * N_DOMAIN + d, to[0] * N_DOMAIN + to[1]))
    return out


def send(array, target):
    return lax.ppermute(array, MESH, pairs(target))


def swap_cores(array):
    return send(array, lambda m, d: (m, d ^ 1))


def over_y(arrays):
    return [send(array, lambda m, d, k=k: (m ^ k, d)) for k, array in zip(STEPS, arrays)]


def over_z_hi(array):
    return send(array, lambda m, d: (m ^ 4, d))


def over_x(array):
    return [send(array, lambda m, d, x=x: (m, d ^ (4 * x))) for x in (1, 2, 3)]


def vmem():
    return pl.BlockSpec(memory_space=pltpu.VMEM)


def hbm():
    return pl.BlockSpec(memory_space=pltpu.HBM)


def shaped(*rows):
    return [pltpu.VMEM((r, SIZE), F32) for r in rows]


def on(space, *arrays):
    return [pltpu.with_memory_space_constraint(x, space) for x in arrays]


def limit(mib):
    return pltpu.CompilerParams(vmem_limit_bytes=mib << 20)


def here():
    return lax.axis_index("member"), lax.axis_index("domain")


def prepare_kernel(owner_hbm, ens_hbm, ctl_hbm, keep, give0, give1, give2, stay, leave, ens, ctl, part, tile, turned, lines, edge, owner, sems, osem):
    member, patch = here()
    z = (patch // 2) % 2
    table = pltpu.make_async_copy(owner_hbm, owner, osem)
    table.start()
    copies = []
    for i in range(PLANES):
        a = pltpu.make_async_copy(ens_hbm.at[:, i], ens.at[:, i], sems.at[0, i])
        b = pltpu.make_async_copy(ctl_hbm.at[i], ctl.at[i], sems.at[1, i])
        a.start()
        b.start()
        copies.append((a, b))
    table.wait()
    flag = jnp.where(owner[patch] == member, 1.0, 0.0).astype(F32)
    for i in range(PLANES):
        for c in copies[i]:
            c.wait()
        spots = [(a // 2, (a % 2) * PLANES + i) for a in range(LOCAL)] + [(0, 24 + i) if i < 8 else (1, 16 + i)]
        for r in range(0, SIZE, 32):
            rows = pl.ds(r, 32)
            group = lax.broadcasted_iota(jnp.int32, (32, SIZE), 1) // 4
            xs = [ens[a, i, rows, :] for a in range(LOCAL)]
            total = (xs[0] + xs[1]) + (xs[2] + xs[3])
            value = flag * ctl[i, rows, :] - total * (1.0 / MEMBERS)
            part[pl.ds(i * SIZE + r, 32), :] = value
            for t in (0, 1):
                acc = tile[t, rows, :]
                for (where, s), x in zip(spots, xs + [value]):
                    if where == t:
                        acc = jnp.where(group == s, pltpu.roll(x, (4 * s + 2) % SIZE, 1), acc)
                tile[t, rows, :] = acc
        for side, k, row in ((0, 0, 0), (0, 1, 1), (1, 0, SIZE - 1), (1, 1, SIZE - 2)):
            at = k * PLANES + i
            if at < TAKEN:
                for a in range(LOCAL):
                    lines[a, side, at : at + 1, :] = ens[a, i, row : row + 1, :]
                edge[side, at : at + 1, :] = part[i * SIZE + row : i * SIZE + row + 1, :]
    turned[0] = tile[0].T
    turned[1] = tile[1].T
    for side, k, q in ((2, 0, 2), (2, 1, 3), (3, 0, 1), (3, 1, 0)):
        count = 8 if k else PLANES
        at = k * PLANES
        for a in range(LOCAL):
            lines[a, side, at : at + count, :] = turned[a // 2, pl.ds((a % 2) * 48 + q, count, stride=4), :]
        edge[side, at : at + 8, :] = turned[0, pl.ds(96 + q, 8, stride=4), :]
        if k == 0:
            edge[side, 8:12, :] = turned[1, pl.ds(96 + q, 4, stride=4), :]
    for out, who in ((stay, z), (leave, 1 - z)):
        for c in (0, 1):
            for side in range(4):
                at = c * RECORD + side * SLOT
                out[at : at + TAKEN, :] = lines[2 * c + who, side, 0:TAKEN, :]
                out[at + 20 : at + 30, :] = edge[side, 10 * c : 10 * c + 10, :]
                out[at + 30 : at + 32, :] = jnp.zeros((2, SIZE), F32)
    for step, out in zip((0,) + STEPS, (keep, give0, give1, give2)):
        for half in (0, 1):
            at = pl.multiple_of(half * HALF + (member % 4 ^ step) * CHUNK, 8)
            out[half * CHUNK : (half + 1) * CHUNK, :] = part[pl.ds(at, CHUNK), :]


def prepare(owner, ensemble, control):
    return pl.pallas_call(
        prepare_kernel,
        out_shape=shaped(*[2 * CHUNK] * 4, 2 * RECORD, 2 * RECORD),
        in_specs=[hbm()] * 3,
        out_specs=[vmem()] * 6,
        scratch_shapes=[
            pltpu.VMEM((LOCAL, PLANES, SIZE, SIZE), F32),
            pltpu.VMEM((PLANES, SIZE, SIZE), F32),
            pltpu.VMEM((ROWS, SIZE), F32),
            pltpu.VMEM((2, SIZE, SIZE), F32),
            pltpu.VMEM((2, SIZE, SIZE), F32),
            pltpu.VMEM((LOCAL, 4, 24, SIZE), F32),
            pltpu.VMEM((4, 24, SIZE), F32),
            pltpu.SMEM((N_DOMAIN,), jnp.int32),
            pltpu.SemaphoreType.DMA((2, PLANES)),
            pltpu.SemaphoreType.DMA,
        ],
        compiler_params=limit(12),
        cost_estimate=pl.CostEstimate(flops=2_000_000, bytes_accessed=5_000_000, transcendentals=0),
        name="prepare",
    )(*on(pltpu.HBM, owner, ensemble, control))


def small(kernel, name, rows, arrays):
    one = isinstance(rows, int)
    return pl.pallas_call(
        kernel,
        out_shape=shaped(rows)[0] if one else shaped(*rows),
        in_specs=[vmem()] * len(arrays),
        out_specs=vmem() if one else [vmem()] * len(rows),
        compiler_params=limit(4),
        name=name,
    )(*on(pltpu.VMEM, *arrays))


def sum_kernel(*refs):
    *terms, out = [r[...] for r in refs[:-1]] + [refs[-1]]
    while len(terms) > 1:
        terms = [terms[i] + terms[i + 1] if i + 1 < len(terms) else terms[i] for i in range(0, len(terms), 2)]
    out[...] = terms[0]


def split_kernel(stay, came, out):
    _, patch = here()
    rows = pl.ds(pl.multiple_of((1 - patch % 2) * RECORD, 8), RECORD)
    out[0:RECORD, :] = stay[rows, :]
    out[RECORD:, :] = came[rows, :]


def group_kernel(stay, came, got, out):
    _, patch = here()
    rows = pl.ds(pl.multiple_of((patch % 2) * RECORD, 8), RECORD)
    out[0:RECORD, :] = stay[rows, :]
    out[RECORD : 2 * RECORD, :] = got[0:RECORD, :]
    out[2 * RECORD : 3 * RECORD, :] = came[rows, :]
    out[3 * RECORD :, :] = got[RECORD:, :]


def pick_kernel(near_hbm, codes_hbm, g0, g1, g3, g2, stay, stay_sib, leave, half, half_sib, near, codes, sems):
    _, patch = here()
    copies = [
        pltpu.make_async_copy(near_hbm, near, sems.at[0]),
        pltpu.make_async_copy(codes_hbm, codes, sems.at[1]),
    ]
    for copy in copies:
        copy.start()
    for copy in copies:
        copy.wait()
    for q in range(4):
        to, base, rows = ((stay, 0, SLOT), (stay_sib, 0, SLOT), (leave, 0, 24), (leave, STRIP, 24))[q]
        for side in range(4):
            away = near[side, patch ^ q] ^ patch
            code = codes[side, patch ^ q]
            source = pl.ds(pl.multiple_of((away % 4) * RECORD + (code % 4) * SLOT, 8), rows)
            value = g0[source, :]
            for x, g in ((1, g1), (2, g2), (3, g3)):
                value = jnp.where(away // 4 == x, g[source, :], value)
            lane = lax.broadcasted_iota(jnp.int32, value.shape, 1)
            value = jnp.take_along_axis(value, jnp.where(code // 4 == 1, SIZE - 1 - lane, lane), axis=1)
            at, depth = base + side * USED, 16 if side < 2 else 12
            to[at : at + PLANES, :] = value[0:PLANES]
            to[at + PLANES : at + USED, :] = value[depth : depth + LEV]
            if q < 2:
                to_half = (half, half_sib)[q]
                to_half[at : at + 10, :] = value[20:30]
                to_half[at + 10 : at + USED, :] = jnp.zeros((6, SIZE), F32)


def pick(neighbours, codes, g0, g1, g2, g3):
    return pl.pallas_call(
        pick_kernel,
        out_shape=shaped(STRIP, STRIP, 2 * STRIP, STRIP, STRIP),
        in_specs=[hbm()] * 2 + [vmem()] * 4,
        out_specs=[vmem()] * 5,
        scratch_shapes=[pltpu.SMEM((4, N_DOMAIN), jnp.int32)] * 2 + [pltpu.SemaphoreType.DMA((2,))],
        compiler_params=limit(4),
        name="pick",
    )(*on(pltpu.HBM, neighbours, codes), *on(pltpu.VMEM, g0, g1, g3, g2))


def merge_kernel(half, came, out):
    _, patch = here()
    first = patch % 2 == 0
    for side in range(4):
        at = side * USED
        mine, other = half[at : at + USED, :], came[at : at + USED, :]
        low, high = jnp.where(first, mine, other), jnp.where(first, other, mine)
        depth = 6 if side < 2 else 2
        out[at : at + 10, :] = low[0:10]
        out[at + 10 : at + 12, :] = high[0:2]
        out[at + 12 : at + 16, :] = high[depth : depth + LEV]


def couple_kernel(stay, back, out):
    out[0:STRIP, :] = stay[...]
    out[STRIP:, :] = back[STRIP:, :]


def slope(x):
    lane = lax.broadcasted_iota(jnp.int32, x.shape, 1)
    ahead = jnp.where(lane == SIZE - 1, 0.0, pltpu.roll(x, SIZE - 1, 1))
    behind = jnp.where(lane == 0, 0.0, pltpu.roll(x, 1, 1))
    return ahead - behind


def recentre_kernel(ens_hbm, own, c, b, a, out, slopes, ens, shift, sems):
    copies = [pltpu.make_async_copy(ens_hbm.at[n], ens.at[n], sems.at[n]) for n in range(LOCAL)]
    for copy in copies:
        copy.start()
    member, _ = here()
    for step, m in zip((0,) + STEPS, (own, a, b, c)):
        for half in (0, 1):
            at = pl.multiple_of(half * HALF + (member % 4 ^ step) * CHUNK, 8)
            shift[pl.ds(at, CHUNK), :] = m[half * CHUNK : (half + 1) * CHUNK, :]
    for n in range(LOCAL):
        copies[n].wait()
        for i in range(PLANES):
            out[n, i, 0:8, :] = jnp.zeros((8, SIZE), F32)
            out[n, i, 8 + SIZE :, :] = jnp.zeros((8, SIZE), F32)
            for r in range(0, SIZE, 32):
                value = ens[n, i, r : r + 32, :] + shift[i * SIZE + r : i * SIZE + r + 32, :]
                out[n, i, 8 + r : 40 + r, :] = value
                slopes[n, i, r : r + 32, :] = slope(value)


def recentre(ensemble, arrays):
    return pl.pallas_call(
        recentre_kernel,
        out_shape=[
            pltpu.VMEM((LOCAL, PLANES, SIZE + 16, SIZE), F32),
            pltpu.VMEM((LOCAL, PLANES, SIZE, SIZE), F32),
        ],
        in_specs=[hbm()] + [vmem()] * len(arrays),
        out_specs=[vmem()] * 2,
        scratch_shapes=[
            pltpu.VMEM((LOCAL, PLANES, SIZE, SIZE), F32),
            pltpu.VMEM((ROWS, SIZE), F32),
            pltpu.SemaphoreType.DMA((LOCAL,)),
        ],
        compiler_params=limit(12),
        name="recentre",
    )(*on(pltpu.HBM, ensemble), *on(pltpu.VMEM, *arrays))


def advance_kernel(fields, slopes, stay, back, got, edge0, edge1, out, rims, lines, columns, div, slope_u):
    now_at = pl.program_id(0)

    @pl.when(now_at == 0)
    def _():
        _, patch = here()
        core, z = patch % 2, (patch // 2) % 2
        for side in range(4):
            rows = slice(side * USED, (side + 1) * USED)
            moved = edge0[rows, :] + edge1[rows, :]
            for source, who in (
                (stay[rows, :], 2 * core + z),
                (back[rows, :], 2 * core + 1 - z),
                (got[rows, :], 2 - 2 * core + z),
                (got[STRIP + side * USED : STRIP + (side + 1) * USED, :], 3 - 2 * core - z),
            ):
                rims[who, side] = source + moved
        for n in range(LOCAL):
            at = n * 32
            lines[pl.ds(at, PLANES, stride=2), :] = rims[n, 3, 0:PLANES, :]
            lines[pl.ds(at + 1, PLANES, stride=2), :] = -rims[n, 2, 0:PLANES, :]
            right = 0.5 * (rims[n, 3, PLANES:USED, :] + slope(rims[n, 3, LEV : 2 * LEV, :]))
            left = 0.5 * (slope(rims[n, 2, LEV : 2 * LEV, :]) - rims[n, 2, PLANES:USED, :])
            lines[pl.ds(at + 24, LEV, stride=2), :] = right
            lines[pl.ds(at + 25, LEV, stride=2), :] = left
        turned = lines[...].T
        for n in range(LOCAL):
            columns[n] = turned if n == 0 else pltpu.roll(turned, SIZE - 32 * n, 1)

    step = now_at
    part = 32
    lane = lax.broadcasted_iota(jnp.int32, (part, SIZE), 1)
    row = lax.broadcasted_iota(jnp.int32, (part, SIZE), 0)
    at_left, at_right = lane == 0, lane == SIZE - 1

    def rows_at(i, r):
        return fields[step, i, 8 + r : 8 + r + part, :]

    def above(i, r):
        value = fields[step, i, 7 + r : 7 + r + part, :]
        return jnp.where(row == 0, rims[step, 0, i : i + 1, :], value) if r == 0 else value

    def below(i, r):
        value = fields[step, i, 9 + r : 9 + r + part, :]
        return jnp.where(row == part - 1, rims[step, 1, i : i + 1, :], value) if r == SIZE - part else value

    at_end = jnp.logical_or(at_left, at_right)

    def across(i, r):
        edge = pltpu.roll(columns[step, r : r + part, :], (SIZE - 1 - 2 * i) % SIZE, 1)
        return slopes[step, i, r : r + part, :] + jnp.where(at_end, edge, 0.0)

    for lev in range(LEV):
        iu, iv, iw, deep = lev, LEV + lev, 2 * LEV + lev, PLANES + lev
        div[7:8, :] = 0.5 * (
            slope(rims[step, 0, iu : iu + 1, :]) + fields[step, iv, 8:9, :] - rims[step, 0, deep : deep + 1, :]
        )
        div[8 + SIZE : 9 + SIZE, :] = 0.5 * (
            slope(rims[step, 1, iu : iu + 1, :])
            + rims[step, 1, deep : deep + 1, :]
            - fields[step, iv, 7 + SIZE : 8 + SIZE, :]
        )
        for r in range(0, SIZE, part):
            du = across(iu, r)
            slope_u[r : r + part, :] = du
            div[8 + r : 8 + r + part, :] = 0.5 * (du + below(iv, r) - above(iv, r))
        for r in range(0, SIZE, part):
            u, v, w = rows_at(iu, r), rows_at(iv, r), rows_at(iw, r)
            edge = pltpu.roll(columns[step, r : r + part, :], (SIZE - 1 - 2 * deep) % SIZE, 1)
            edge = edge + jnp.where(at_left, 0.5 * u, -0.5 * u)
            mid = div[8 + r : 8 + r + part, :]
            grad_x = jnp.where(at_right, edge, pltpu.roll(mid, SIZE - 1, 1)) - jnp.where(at_left, edge, pltpu.roll(mid, 1, 1))
            grad_y = div[9 + r : 9 + r + part, :] - div[7 + r : 7 + r + part, :]
            new_u = u - 0.2 * (u * slope_u[r : r + part, :] + v * (below(iu, r) - above(iu, r)))
            new_v = v - 0.2 * (u * across(iv, r) + v * (below(iv, r) - above(iv, r)))
            new_w = w - 0.2 * (u * across(iw, r) + v * (below(iw, r) - above(iw, r)))
            out[0, iu, r : r + part, :] = new_u + 0.1 * grad_x
            out[0, iv, r : r + part, :] = new_v + 0.1 * grad_y
            out[0, iw, r : r + part, :] = new_w


def advance(*arrays):
    return pl.pallas_call(
        advance_kernel,
        out_shape=jax.ShapeDtypeStruct((LOCAL, PLANES, SIZE, SIZE), F32),
        grid=(LOCAL,),
        in_specs=[vmem()] * len(arrays),
        out_specs=pl.BlockSpec((1, PLANES, SIZE, SIZE), lambda n: (n, 0, 0, 0)),
        scratch_shapes=[
            pltpu.VMEM((LOCAL, 4, USED, SIZE), F32),
            pltpu.VMEM((SIZE, SIZE), F32),
            pltpu.VMEM((LOCAL, SIZE, SIZE), F32),
            pltpu.VMEM((SIZE + 16, SIZE), F32),
            pltpu.VMEM((SIZE, SIZE), F32),
        ],
        compiler_params=limit(8),
        cost_estimate=pl.CostEstimate(flops=40_000_000, bytes_accessed=8_000_000, transcendentals=0),
        name="advance",
    )(*on(pltpu.VMEM, *arrays))


def on_device(ensemble, control, owner, neighbours, codes):
    shape = ensemble.shape
    ensemble = ensemble.reshape(LOCAL, PLANES, SIZE, SIZE)
    control = control.reshape(PLANES, SIZE, SIZE)

    keep, *gives, stay, leave = prepare(owner, ensemble, control)
    strips = send(leave, lambda m, d: (m, d ^ 2))
    halves = swap_cores(small(split_kernel, "split", 2 * RECORD, [stay, strips]))
    group = small(group_kernel, "group", 4 * RECORD, [stay, strips, halves])
    total = small(sum_kernel, "total", 2 * CHUNK, [*over_y(gives), keep])
    total = small(sum_kernel, "shift", 2 * CHUNK, [total, over_z_hi(total)])
    chunks = over_y([total] * 3)
    stay, stay_sib, leave, half, half_sib = pick(neighbours.T, codes.T, group, *over_x(group))
    came = swap_cores(half_sib)
    back = send(leave, lambda m, d: (m, d ^ 2))
    got = swap_cores(small(couple_kernel, "couple", 2 * STRIP, [stay_sib, back]))
    edge = small(merge_kernel, "merge", STRIP, [half, came])
    edge = small(sum_kernel, "edge", STRIP, [edge, over_z_hi(edge)])
    edge = small(sum_kernel, "edge", STRIP, [edge, send(edge, lambda m, d: (m ^ 1, d))])
    other = send(edge, lambda m, d: (m ^ 3, d))
    fields, slopes = recentre(ensemble, [total, *chunks[::-1]])
    out = advance(fields, slopes, stay, back, got, edge, other)
    return out.reshape(shape)


def solution(mesh):
    spec = P("member", None, None, "domain", None)
    return jax.shard_map(
        on_device, mesh=mesh, in_specs=(spec, spec, P(), P(), P()), out_specs=spec, check_vma=False
    )
```
